512 devices in a mesh: ctx: 16 (over z_lo, core), exp: 32 (over z_hi, x, y).
Axes of the slice: x: 4, y: 4, z: 16 (z_hi: 2, z_lo: 8; z = z_hi * 8 + z_lo), core: 2. Of those that a mesh axis runs over, the one named last changes fastest.
Arguments:
- residual: bfloat16 [32, 2048, 1024], P('exp', 'ctx'), may hold values from -6 to 6
- query_rows: bfloat16 [32, 2048, 1024], P('exp', 'ctx'), may hold values from -8 to 8
- key_rows: bfloat16 [32, 2048, 1024], P('exp', 'ctx'), may hold values from -4 to 4
- value_rows: bfloat16 [32, 2048, 1024], P('exp', 'ctx'), may hold values from -6 to 6
- out_proj: bfloat16 [1024, 1024], P('exp'), may hold values from -0.75 to 0.75
- router: bfloat16 [1024, 32], replicated, may hold values from -0.5 to 0.5
- expert_ids: int32 [32, 2048, 2], P('exp', 'ctx'), may hold values from 0 to 31, all different within a row; in each aligned block of 128 rows (0 to 127, 128 to 255, ..., all dimensions but the last counted through in order) at most 12 rows name the same one
- expert_gate_up: bfloat16 [32, 1024, 1536], P('exp', 'ctx'), may hold values from -0.1875 to 0.1875
- expert_down: bfloat16 [32, 768, 1024], P('exp', 'ctx'), may hold values from -0.21875 to 0.21875
Outputs:
- layer_out: bfloat16 [32, 2048, 1024], P('exp', 'ctx')
The draws below stay inside these ranges and needn't reach their ends.
Inputs may be any that keep to these rules, and one draw needn't show every extreme that they name: `expert_ids`: the 2 ids of a token differ. Among the 128 tokens of one device (aligned blocks of 128 tokens of the flattened sequences) each expert is named at most 12 times, a bound that some block reaches.
All inputs are finite; a program needn't handle non-finite values.
Results may differ from the reference program's by a relative error of at most 0.017.
Values may be sent and summed in bfloat16 or wider, within the bound.
No kernel may reach another device: no remote copies, remote signals or barrier semaphores. Data moves between devices by JAX's collectives and lax.ppermute only.
A program may use at most 64 MiB of HBM per device.

```python
import math
import jax
import jax.numpy as jnp
import numpy as np
from jax import lax

D = 1024
HEADS = 8
HEAD_DIM = 128
FF = 768
TOP = 2
TOK_DEV = 128
HD = 1024
SEQ_LEN = 2048
SEQS = 32
EXPERTS = 32
CAP = 12
N_CTX = 16
N_EXP = 32


def draw_query_rows(key, part):
    sample = 2.0 * jnp.clip(jax.random.normal(jax.random.fold_in(key, 1), (SEQS, SEQ_LEN, HD), jnp.float32), -4.0, 4.0)
    return sample.astype(jnp.bfloat16)


def draw_key_rows(key, part):
    sample = jnp.clip(jax.random.normal(jax.random.fold_in(key, 2), (SEQS, SEQ_LEN, HD), jnp.float32), -4.0, 4.0)
    return sample.astype(jnp.bfloat16)


def block_scale(stream_key, shape, split, smallest, largest):
    loudness = 1.0
    for dim, blocks in split:
        heights = jax.random.uniform(jax.random.fold_in(jax.random.fold_in(stream_key, 6), dim), (blocks,), jnp.float32, smallest / len(split), largest / len(split))
        loudness = loudness * jnp.repeat(jnp.exp(heights), shape[dim] // blocks).reshape((-1,) + (1,) * (len(shape) - 1 - dim))
    return loudness


def routed_block(own_key, own, number, rows, count, top, bound, skew):
    order = jax.random.permutation(own_key, count)
    packed, ordinary = portions_of(count, rows * top, bound, skew, True), portions_of(count, rows * top, bound, skew, False)
    places = jnp.arange(count)

    def named(sizes, turn):
        used = int((sizes > 0).sum())
        fixed = max(1, used // 4)
        passed = fixed + (places - fixed + turn * (used - fixed)) % max(1, count - fixed)
        return jnp.zeros((count,), jnp.int32).at[order[jnp.where(places < fixed, places, passed)]].set(jnp.asarray(sizes, jnp.int32))

    sizes = jnp.where(number % 4 == 0, named(packed, number // 4), named(ordinary, number - number // 4 - 1))
    mixed = jax.random.permutation(jax.random.fold_in(own, 3), count)
    source_of, receiver = mixed[0:count // 2 * 2:2], mixed[1:count // 2 * 2:2]
    room = jnp.minimum(sizes[source_of] - 1, bound - sizes[receiver]) // 2
    room = jnp.where((source_of == order[0]) | (receiver == order[0]) | (sizes[receiver] == 0), 0, jnp.maximum(room, 0))
    passed = jax.random.randint(jax.random.fold_in(own, 4), (count // 2,), 0, 1 << 20) % (room + 1)
    sizes = sizes.at[source_of].add(-passed).at[receiver].add(passed)
    items = jnp.searchsorted(jnp.cumsum(sizes), jnp.arange(rows * top), side="right").astype(jnp.int32)
    listing = items.reshape(top, rows).T
    listing = listing[jax.random.permutation(jax.random.fold_in(own, 1), rows)]
    turn = jax.random.randint(jax.random.fold_in(own, 2), (rows, 1), 0, top)
    return jnp.take_along_axis(listing, (jnp.arange(top)[None, :] + turn) % top, axis=1)


def portions_of(count, total, reach, skew, full):
    loads = [(1 << 20) // math.isqrt(rank ** skew) + 1 for rank in range(1, count + 1)]
    largest = reach if full else min(reach, max(-(-total // count), total * loads[0] // sum(loads)))
    least = 1 if total - largest >= count - 1 else 0
    counts, surplus = [largest] + [least] * (count - 1), total - largest - least * (count - 1)
    while surplus > 0:
        free = [i for i in range(1, count) if counts[i] < largest] or [i for i in range(1, count) if counts[i] < reach]
        pool, budget = sum([loads[i] for i in free]), surplus
        for i in free:
            addition = min(reach - counts[i], max(1, budget * loads[i] // pool), surplus)
            counts[i] = counts[i] + addition
            surplus = surplus - addition
    return np.array(counts)


def bell_draw(rng, shape, spread, bound, cuts=(), held_as=jnp.bfloat16):
    entries = jax.random.normal(rng, shape, jnp.float32) * spread
    if len(cuts) > 0:
        entries = block_scale(rng, shape, cuts, -0.22, 0.18) * entries
    return jnp.clip(entries, min=-bound, max=bound).astype(held_as)


def setup_inputs(seed: int = 0) -> dict:
    seeds = jax.random.split(jax.random.key(seed), 10)
    residual = bell_draw(seeds[0], (SEQS, SEQ_LEN, D), 1.0, 6.0, ((0, 32), (1, 16)))
    query_rows = draw_query_rows(jax.random.fold_in(seeds[9], 71), 0)
    key_rows = draw_key_rows(jax.random.fold_in(seeds[9], 71), 0)
    value_rows = bell_draw(seeds[3], (SEQS, SEQ_LEN, HD), 1.0, 6.0, ((0, 32), (1, 16)))
    out_proj = bell_draw(seeds[4], (HD, D), (HD // 16) ** -0.5, 0.75, ((0, 32),))
    router = bell_draw(seeds[5], (D, EXPERTS), (D // 9) ** -0.5, 0.5)
    expert_ids_keys = jax.random.split(jax.random.fold_in(seeds[6], 1), SEQS * SEQ_LEN // TOK_DEV)
    expert_ids_turns = jax.random.permutation(jax.random.fold_in(seeds[6], 3), SEQS * SEQ_LEN // TOK_DEV)
    expert_ids = jax.vmap(lambda own, number: routed_block(jax.random.fold_in(seeds[6], 2), own, number, TOK_DEV, EXPERTS, TOP, CAP, 2))(expert_ids_keys, expert_ids_turns).reshape((SEQS, SEQ_LEN, TOP))
    expert_gate_up = bell_draw(seeds[7], (EXPERTS, D, 2 * FF), D ** -0.5, 0.1875, ((0, 32), (1, 16)))
    expert_down = bell_draw(seeds[8], (EXPERTS, FF, D), FF ** -0.5, 0.21875, ((0, 32), (1, 16)))
    return dict(residual=residual, query_rows=query_rows, key_rows=key_rows, value_rows=value_rows, out_proj=out_proj, router=router, expert_ids=expert_ids, expert_gate_up=expert_gate_up, expert_down=expert_down)


NEG_FILL = -1e+30

def attend_sequence(operands):
    query_seq, key_seq, value_seq = operands
    length = query_seq.shape[0]
    scale_factor = HEAD_DIM ** (-0.5)
    query_heads = query_seq.astype(jnp.float32).reshape(length, HEADS, HEAD_DIM).transpose(1, 0, 2)
    key_heads = key_seq.astype(jnp.float32).reshape(length, HEADS, HEAD_DIM).transpose(1, 0, 2)
    value_heads = value_seq.astype(jnp.float32).reshape(length, HEADS, HEAD_DIM).transpose(1, 0, 2)
    position = jnp.arange(length)
    allowed = position[None, :] <= position[:, None]

    def one_head(head_operands):
        query_head, key_head, value_head = head_operands
        scores = jnp.dot(query_head, key_head.T, preferred_element_type=jnp.float32) * scale_factor
        row_max = lax.optimization_barrier(jnp.max(jnp.where(allowed, scores, NEG_FILL), axis=1, keepdims=True))
        exp_scores = jnp.where(allowed, jnp.exp(scores - row_max), 0.0)
        denominator = lax.optimization_barrier(jnp.sum(exp_scores, axis=1, keepdims=True))
        prob_bf = lax.optimization_barrier(exp_scores.astype(jnp.bfloat16)).astype(jnp.float32)
        return jnp.dot(prob_bf, value_head, preferred_element_type=jnp.float32) / denominator
    per_head = lax.map(one_head, (query_heads, key_heads, value_heads))
    return per_head.transpose(1, 0, 2).reshape(length, HEADS * HEAD_DIM).astype(jnp.bfloat16)

def reference(residual, query_rows, key_rows, value_rows, out_proj, router, expert_ids, expert_gate_up, expert_down):
    context = lax.map(attend_sequence, (query_rows, key_rows, value_rows))
    token_total = SEQS * SEQ_LEN
    attn_out = jnp.dot(context.reshape(token_total, HEADS * HEAD_DIM), out_proj, preferred_element_type=jnp.float32)
    hidden_state = (residual.reshape(token_total, D).astype(jnp.float32) + attn_out).astype(jnp.bfloat16)
    hidden_wide = hidden_state.astype(jnp.float32)
    mean_square = lax.optimization_barrier(jnp.mean(hidden_wide * hidden_wide, axis=1, keepdims=True))
    normed = (hidden_wide * lax.rsqrt(mean_square + 1e-06)).astype(jnp.bfloat16)
    affinity = jax.nn.sigmoid(jnp.dot(normed, router, preferred_element_type=jnp.float32))
    chosen_ids = expert_ids.reshape(token_total, TOP).astype(jnp.int32)
    picked = jnp.take_along_axis(affinity, chosen_ids, axis=1)
    gate_share = picked / lax.optimization_barrier(jnp.sum(picked, axis=1, keepdims=True))
    pair_ids = chosen_ids.reshape(token_total * TOP)
    slot_bound = N_EXP * N_CTX * CAP

    def one_expert(expert, collected):
        members = jnp.nonzero(pair_ids == expert, size=slot_bound, fill_value=token_total * TOP)[0].astype(jnp.int32)
        token_index = jnp.minimum(members // TOP, token_total - 1).astype(jnp.int32)
        token_feats = jnp.take(normed, token_index, axis=0)
        gate_up_out = jnp.dot(token_feats, expert_gate_up[expert], preferred_element_type=jnp.float32)
        activation = (jax.nn.silu(gate_up_out[:, :FF]) * gate_up_out[:, FF:]).astype(jnp.bfloat16)
        produced = jnp.dot(activation, expert_down[expert], preferred_element_type=jnp.float32).astype(jnp.bfloat16)
        return collected.at[members].set(produced, mode='drop')
    collected = lax.fori_loop(0, EXPERTS, one_expert, jnp.zeros((token_total * TOP, D), jnp.bfloat16))
    pair_out = collected.reshape(token_total, TOP, D).astype(jnp.float32)
    moe_out = lax.optimization_barrier(jnp.sum(gate_share[:, :, None] * pair_out, axis=1))
    return (hidden_wide + moe_out).astype(jnp.bfloat16).reshape(SEQS, SEQ_LEN, D)
```

```python
import functools

import jax
import jax.numpy as jnp
from jax import lax
from jax.experimental import pallas as pl
from jax.experimental.pallas import tpu as pltpu
from jax.sharding import Mesh, PartitionSpec as P

HEADS = 8
HEAD_DIM = 128
TOP = 2
SLOT = 16
NEG_FILL = -1e30
LOG2E = 1.4426950408889634
BF = jnp.bfloat16
F32 = jnp.float32
ALL = ("zlo", "core", "zhi", "xy")

VMEM = pl.BlockSpec(memory_space=pltpu.VMEM)
SMEM = pl.BlockSpec(memory_space=pltpu.SMEM)
ANY = pl.BlockSpec(memory_space=pl.ANY)


def linear(zlo, core, zhi, xy):
    return ((zlo * 2 + core) * 2 + zhi) * 16 + xy


def all_pairs(move):
    pairs = []
    for zlo in range(8):
        for core in range(2):
            for zhi in range(2):
                for xy in range(16):
                    target = move(zlo, core, zhi, xy)
                    if target is not None:
                        pairs.append((linear(zlo, core, zhi, xy), linear(*target)))
    return pairs


CORE_SWAP = all_pairs(lambda zlo, core, zhi, xy: (zlo, 1 - core, zhi, xy))
HALF_MOVE = all_pairs(lambda zlo, core, zhi, xy: (zlo, core, 1 - zhi, xy) if zhi == core else None)


def params(mib):
    return pltpu.CompilerParams(vmem_limit_bytes=mib << 20)


def pack_weights_kernel(up_ref, down_ref, out_ref):
    out_ref[0:64, :] = up_ref[0, :, 0:1024]
    out_ref[64:96, 0:512] = up_ref[0, 0:32, 1024:1536]
    out_ref[64:96, 512:1024] = up_ref[0, 32:64, 1024:1536]
    out_ref[96:144, :] = down_ref[0]


def pack_weights(gate_up, down):
    return pl.pallas_call(
        pack_weights_kernel,
        out_shape=jax.ShapeDtypeStruct((144, 1024), BF),
        in_specs=[VMEM, VMEM],
        out_specs=VMEM,
        compiler_params=params(8),
    )(gate_up, down)


def pack_heads_kernel(q_ref, k_ref, v_ref, out_ref):
    for h in range(HEADS):
        for c in range(2):
            for j, ref in enumerate((q_ref, k_ref, v_ref)):
                out_ref[h * 2 + c, j * 64 : (j + 1) * 64, :] = ref[
                    0, c * 64 : (c + 1) * 64, h * 128 : (h + 1) * 128
                ]


def pack_heads(q, k, v):
    return pl.pallas_call(
        pack_heads_kernel,
        out_shape=jax.ShapeDtypeStruct((16, 192, 128), BF),
        in_specs=[VMEM] * 3,
        out_specs=VMEM,
        compiler_params=params(8),
    )(q, k, v)


def attention_kernel(core_ref, own_ref, oth_ref, out_ref):
    core = core_ref[0]
    queries = own_ref[:, 0:64, :].reshape(1024, 128)
    own_keys = own_ref[:, 64:128, :].reshape(1024, 128)
    own_values = own_ref[:, 128:192, :].reshape(1024, 128)
    oth_keys = oth_ref[:, 0:64, :].reshape(1024, 128)
    oth_values = oth_ref[:, 64:128, :].reshape(1024, 128)
    scale = (HEAD_DIM ** (-0.5)) * LOG2E
    rows = 256
    row = lax.broadcasted_iota(jnp.int32, (rows, rows), 0)
    col = lax.broadcasted_iota(jnp.int32, (rows, rows), 1)
    own_allowed = col <= row
    oth_allowed = (col // 64) < (row // 64) + core
    contract = (((1,), (1,)), ((), ()))
    for j in range(1024 // rows):
        q = queries[j * rows : (j + 1) * rows]
        n = j * rows
        pieces = []
        for keys, values, allowed in (
            (own_keys, own_values, own_allowed),
            (oth_keys, oth_values, oth_allowed),
        ):
            if n:
                s = lax.dot_general(q, keys[:n], contract, preferred_element_type=F32) * scale
                pieces.append((s, values[:n]))
            s = lax.dot_general(q, keys[n : n + rows], contract, preferred_element_type=F32) * scale
            pieces.append((jnp.where(allowed, s, NEG_FILL), values[n : n + rows]))
        top = functools.reduce(jnp.maximum, [jnp.max(s, axis=1, keepdims=True) for s, _ in pieces])
        acc = jnp.zeros((rows, HEAD_DIM), F32)
        total = jnp.zeros((rows, 1), F32)
        for s, values in pieces:
            e = jnp.exp2(s - top)
            total = total + jnp.sum(e, axis=1, keepdims=True)
            acc = acc + jnp.dot(e.astype(BF), values, preferred_element_type=F32)
        out_ref[j * (rows // 64) : (j + 1) * (rows // 64)] = (
            (acc / total).astype(BF).reshape(rows // 64, 64, HEAD_DIM)
        )


def attention(core, own, oth):
    return pl.pallas_call(
        attention_kernel,
        out_shape=jax.ShapeDtypeStruct((16, 64, 128), BF),
        in_specs=[SMEM, VMEM, VMEM],
        out_specs=VMEM,
        compiler_params=params(32),
        cost_estimate=pl.CostEstimate(
            flops=2 * 2 * 1024 * 1280 * 128, bytes_accessed=2 << 20, transcendentals=1024 * 1280
        ),
    )(core, own, oth)


def middle_kernel(
    core_ref, ctx_ref, own_ref, oth_ref, res_ref, router_ref, ids_ref,
    hidden_ref, out_ref, gate_ref, target_ref, halves,
):
    core = core_ref[0]
    for h in range(HEADS):
        for c in range(2):
            halves[h // 4, c * 64 : (c + 1) * 64, (h % 4) * 128 : (h % 4 + 1) * 128] = ctx_ref[h * 2 + c]
    attn = jnp.dot(halves[core], own_ref[...], preferred_element_type=F32)
    attn = attn + jnp.dot(halves[1 - core], oth_ref[...], preferred_element_type=F32)
    hidden = (res_ref[0].astype(F32) + attn).astype(BF)
    hidden_ref[...] = hidden
    wide = hidden.astype(F32)
    mean_square = jnp.mean(wide * wide, axis=1, keepdims=True)
    normed = (wide * lax.rsqrt(mean_square + 1e-06)).astype(BF)
    affinity = jax.nn.sigmoid(jnp.dot(normed, router_ref[...], preferred_element_type=F32))
    tokens, experts = affinity.shape
    ids = ids_ref[0]
    lane = lax.broadcasted_iota(jnp.int32, (tokens, experts), 1)
    hot = [lane == ids[:, k : k + 1] for k in range(TOP)]
    picked = [jnp.sum(jnp.where(m, affinity, 0.0), axis=1, keepdims=True) for m in hot]
    whole = picked[0] + picked[1]
    below = (
        lax.broadcasted_iota(jnp.int32, (tokens, tokens), 1)
        < lax.broadcasted_iota(jnp.int32, (tokens, tokens), 0)
    ).astype(F32).astype(BF)
    counts = jnp.zeros((1, experts), F32)
    slot_lane = lax.broadcasted_iota(jnp.int32, (tokens, experts * SLOT), 1)
    dispatch = jnp.zeros((tokens, experts * SLOT), F32)
    for k in range(TOP):
        one = hot[k].astype(F32)
        rank = jnp.dot(below, one.astype(BF), preferred_element_type=F32) + counts
        slot = jnp.sum(rank * one, axis=1, keepdims=True).astype(jnp.int32)
        counts = counts + jnp.sum(one, axis=0, keepdims=True)
        target = ids[:, k : k + 1] * SLOT + slot
        dispatch = dispatch + (slot_lane == target).astype(F32)
        gate_ref[:, k : k + 1] = picked[k] / whole
        target_ref[:, k : k + 1] = target
    out_ref[...] = lax.dot_general(
        dispatch.astype(BF), normed, (((0,), (0,)), ((), ())), preferred_element_type=F32
    ).astype(BF)


def middle(core, ctx, own, oth, residual, router, ids):
    tokens, width = residual.shape[1:]
    experts = router.shape[1]
    return pl.pallas_call(
        middle_kernel,
        out_shape=(
            jax.ShapeDtypeStruct((tokens, width), BF),
            jax.ShapeDtypeStruct((experts * SLOT, width), BF),
            jax.ShapeDtypeStruct((tokens, TOP), F32),
            jax.ShapeDtypeStruct((tokens, TOP), jnp.int32),
        ),
        in_specs=[SMEM] + [VMEM] * 6,
        out_specs=(VMEM,) * 4,
        scratch_shapes=[pltpu.VMEM((2, 128, 512), BF)],
        compiler_params=params(32),
        cost_estimate=pl.CostEstimate(
            flops=2 * 128 * 1024 * 1600, bytes_accessed=4 << 20, transcendentals=4096
        ),
    )(core, ctx, own, oth, residual, router, ids)


def expert_kernel(core_ref, x_ref, own_ref, oth_ref, out_ref, up, down, sems):
    core = core_ref[0]
    copies = []
    for which in range(2):
        if which == 0:
            source, place = own_ref.at[pl.ds(core * 8, 8)], core
        else:
            source, place = oth_ref, 1 - core
        parts = (
            (source.at[:, 0:64, :], up.at[:, place, :, 0:1024]),
            (source.at[:, 64:96, 0:512], up.at[:, place, 0:32, 1024:1536]),
            (source.at[:, 64:96, 512:1024], up.at[:, place, 32:64, 1024:1536]),
            (source.at[:, 96:144, :], down.at[:, place]),
        )
        for j, (src, dst) in enumerate(parts):
            copies.append(pltpu.make_async_copy(src, dst, sems.at[which * 4 + j]))
    for copy in copies:
        copy.start()
    for j in (0, 1, 2, 4, 5, 6):
        copies[j].wait()
    ff = down.shape[0] * 2 * down.shape[2]
    up_all = up[...].reshape(1024, 2 * ff)
    inner = jnp.dot(x_ref[...], up_all, preferred_element_type=F32)
    activation = (jax.nn.silu(inner[:, :ff]) * inner[:, ff:]).astype(BF)
    for j in (3, 7):
        copies[j].wait()
    out_ref[...] = jnp.dot(
        activation, down[...].reshape(ff, 1024), preferred_element_type=F32
    ).astype(BF)


def experts(core, x, own, oth):
    rows = x.shape[0]
    return pl.pallas_call(
        expert_kernel,
        out_shape=jax.ShapeDtypeStruct((rows, 1024), BF),
        in_specs=[SMEM, VMEM, ANY, ANY],
        out_specs=VMEM,
        scratch_shapes=[
            pltpu.VMEM((8, 2, 64, 1536), BF),
            pltpu.VMEM((8, 2, 48, 1024), BF),
            pltpu.SemaphoreType.DMA((8,)),
        ],
        compiler_params=params(40),
        cost_estimate=pl.CostEstimate(
            flops=2 * rows * 1024 * 2304, bytes_accessed=7 << 20, transcendentals=rows * 768
        ),
    )(core, x, own, oth)


def combine_kernel(back_ref, hidden_ref, gate_ref, target_ref, out_ref):
    tokens = hidden_ref.shape[0]
    lane = lax.broadcasted_iota(jnp.int32, (tokens, back_ref.shape[0]), 1)
    total = hidden_ref[...].astype(F32)
    moe = None
    for k in range(TOP):
        pick = (lane == target_ref[:, k : k + 1]).astype(F32).astype(BF)
        pair = jnp.dot(pick, back_ref[...], preferred_element_type=F32) * gate_ref[:, k : k + 1]
        moe = pair if moe is None else moe + pair
    out_ref[0] = (total + moe).astype(BF)


def combine(back, hidden, gate, target):
    return pl.pallas_call(
        combine_kernel,
        out_shape=jax.ShapeDtypeStruct((1,) + hidden.shape, BF),
        in_specs=[VMEM] * 4,
        out_specs=VMEM,
        compiler_params=params(16),
    )(back, hidden, gate, target)


def on_device(
    residual, query_rows, key_rows, value_rows, out_proj, router, expert_ids,
    expert_gate_up, expert_down,
):
    core_index = lax.axis_index("core")
    core = core_index.astype(jnp.int32).reshape(1)
    packed = pack_weights(expert_gate_up, expert_down)
    weights = lax.all_gather(packed, ("zhi", "zlo"), axis=0, tiled=False)

    moved = lax.ppermute(out_proj, ALL, HALF_MOVE)
    shard = jnp.where(lax.axis_index("zhi") == core_index, out_proj, moved)
    proj_own = lax.all_to_all(
        jnp.broadcast_to(shard[None], (16,) + shard.shape), "xy", split_axis=0, concat_axis=0, tiled=True
    ).reshape(512, 1024)
    proj_oth = lax.ppermute(proj_own, ALL, CORE_SWAP)

    heads = pack_heads(query_rows, key_rows, value_rows)
    heads = lax.all_to_all(heads, ("zlo", "core"), split_axis=0, concat_axis=0, tiled=True)
    oth_heads = lax.ppermute(heads[:, 64:192, :], ALL, CORE_SWAP)
    context = attention(core, heads, oth_heads)
    context = lax.all_to_all(context, ("zlo", "core"), split_axis=0, concat_axis=0, tiled=True)

    hidden, outgoing, gate, target = middle(
        core, context, proj_own, proj_oth, residual, router, expert_ids
    )
    arrived = lax.all_to_all(
        outgoing.reshape(32, SLOT, 1024), ("core", "xy"), split_axis=0, concat_axis=0, tiled=True
    )
    to_send = lax.dynamic_slice_in_dim(weights, (1 - core_index) * 8, 8, axis=0)
    oth_weights = lax.ppermute(to_send, ALL, CORE_SWAP)
    produced = experts(core, arrived.reshape(32 * SLOT, 1024), weights, oth_weights)
    back = lax.all_to_all(
        produced.reshape(32, SLOT, 1024), ("core", "xy"), split_axis=0, concat_axis=0, tiled=True
    )
    return combine(back.reshape(32 * SLOT, 1024), hidden, gate, target)


def solution(mesh):
    fine = Mesh(mesh.devices.reshape(8, 2, 2, 16), ALL)
    rows = P(("zhi", "xy"), ("zlo", "core"), None)
    return jax.shard_map(
        on_device,
        mesh=fine,
        in_specs=(rows, rows, rows, rows, P(("zhi", "xy"), None), P(), rows, rows, rows),
        out_specs=rows,
        check_vma=False,
    )
```

```python
import functools

import jax
import jax.numpy as jnp
from jax import lax
from jax.experimental import pallas as pl
from jax.experimental.pallas import tpu as pltpu
from jax.sharding import Mesh, PartitionSpec as P

HEADS = 8
HEAD_DIM = 128
TOP = 2
SLOT = 16
PART = 2
NEG_FILL = -1e30
LOG2E = 1.4426950408889634
BF = jnp.bfloat16
F32 = jnp.float32
ALL = ("zlo", "core", "zhi", "xy")

VMEM = pl.BlockSpec(memory_space=pltpu.VMEM)
SMEM = pl.BlockSpec(memory_space=pltpu.SMEM)
ANY = pl.BlockSpec(memory_space=pl.ANY)
HBM = pl.BlockSpec(memory_space=pltpu.HBM)


def linear(zlo, core, zhi, xy):
    return ((zlo * 2 + core) * 2 + zhi) * 16 + xy


def all_pairs(move):
    pairs = []
    for zlo in range(8):
        for core in range(2):
            for zhi in range(2):
                for xy in range(16):
                    target = move(zlo, core, zhi, xy)
                    if target is not None:
                        pairs.append((linear(zlo, core, zhi, xy), linear(*target)))
    return pairs


CORE_SWAP = all_pairs(lambda zlo, core, zhi, xy: (zlo, 1 - core, zhi, xy))
HALF_MOVE = all_pairs(lambda zlo, core, zhi, xy: (zlo, core, 1 - zhi, xy) if zhi == core else None)


def plane_pairs(phase, step):
    def move(zlo, core, zhi, xy):
        x, y = divmod(xy, 4)
        if (phase + core) % 2 == 0:
            x = (x - step) % 4
        else:
            y = (y - step) % 4
        return zlo, core, zhi, x * 4 + y

    return all_pairs(move)


def params(mib):
    return pltpu.CompilerParams(vmem_limit_bytes=mib << 20)


def copy_kernel(plan, n_in, n_out, *refs):
    ins, outs, sems = refs[:n_in], refs[n_in : n_in + n_out], refs[-1]
    copies = [pltpu.make_async_copy(a, b, sems.at[n]) for n, (a, b) in enumerate(plan(ins, outs))]
    for copy in copies:
        copy.start()
    for copy in copies:
        copy.wait()


def copies_call(plan, count, outs, *operands, order=(), mib=56, bytes_accessed=2 << 20):
    many = isinstance(outs, tuple)
    return pl.pallas_call(
        functools.partial(copy_kernel, plan, len(operands) + len(order), len(outs) if many else 1),
        out_shape=outs,
        in_specs=[HBM] * len(operands) + [ANY] * len(order),
        out_specs=(HBM,) * len(outs) if many else HBM,
        scratch_shapes=[pltpu.SemaphoreType.DMA((count,))],
        compiler_params=params(mib),
        cost_estimate=pl.CostEstimate(flops=0, bytes_accessed=bytes_accessed, transcendentals=0),
    )(*operands, *order)


def heads_plan(ins, outs):
    return [
        (ref.at[:, :, h * 128 : (h + 1) * 128], outs[0].at[h, :, j * 64 : (j + 1) * 64, :])
        for h in range(HEADS)
        for j, ref in enumerate(ins[:3])
    ]


def weights_plan(ins, outs):
    up, down = ins
    return [
        (up.at[:, 0:1024], outs[0].at[0:64, :]),
        (up.at[0:32, 1024:1536], outs[0].at[64:96, 0:512]),
        (up.at[32:64, 1024:1536], outs[0].at[64:96, 512:1024]),
        (down, outs[0].at[96:144, :]),
    ]


def keys_plan(ins, outs):
    return [(ins[0].at[:, 64:192, :], outs[0])]


def attention_kernel(core_ref, own_ref, oth_ref, out_ref):
    core = core_ref[0]
    queries = own_ref[:, 0:64, :].reshape(1024, 128)
    own_keys = own_ref[:, 64:128, :].reshape(1024, 128)
    own_values = own_ref[:, 128:192, :].reshape(1024, 128)
    oth_keys = oth_ref[:, 0:64, :].reshape(1024, 128)
    oth_values = oth_ref[:, 64:128, :].reshape(1024, 128)
    scale = (HEAD_DIM ** (-0.5)) * LOG2E
    rows = 256
    row = lax.broadcasted_iota(jnp.int32, (rows, rows), 0)
    col = lax.broadcasted_iota(jnp.int32, (rows, rows), 1)
    own_allowed = col <= row
    oth_allowed = (col // 64) < (row // 64) + core
    contract = (((1,), (1,)), ((), ()))
    for j in range(1024 // rows):
        q = queries[j * rows : (j + 1) * rows]
        n = j * rows
        pieces = []
        for keys, values, allowed in (
            (own_keys, own_values, own_allowed),
            (oth_keys, oth_values, oth_allowed),
        ):
            if n:
                s = lax.dot_general(q, keys[:n], contract, preferred_element_type=F32) * scale
                pieces.append((s, values[:n]))
            s = lax.dot_general(q, keys[n : n + rows], contract, preferred_element_type=F32) * scale
            pieces.append((jnp.where(allowed, s, NEG_FILL), values[n : n + rows]))
        top = functools.reduce(jnp.maximum, [jnp.max(s, axis=1, keepdims=True) for s, _ in pieces])
        acc = jnp.zeros((rows, HEAD_DIM), F32)
        total = jnp.zeros((rows, 1), F32)
        for s, values in pieces:
            e = jnp.exp2(s - top)
            total = total + jnp.sum(e, axis=1, keepdims=True)
            acc = acc + jnp.dot(e.astype(BF), values, preferred_element_type=F32)
        out_ref[j * (rows // 64) : (j + 1) * (rows // 64)] = (
            (acc / total).astype(BF).reshape(rows // 64, 64, HEAD_DIM)
        )


def attention(core, own, oth):
    return pl.pallas_call(
        attention_kernel,
        out_shape=jax.ShapeDtypeStruct((16, 64, 128), BF),
        in_specs=[SMEM, VMEM, VMEM],
        out_specs=VMEM,
        compiler_params=params(20),
        cost_estimate=pl.CostEstimate(
            flops=2 * 2 * 1024 * 1280 * 128, bytes_accessed=2 << 20, transcendentals=1024 * 1280
        ),
    )(core, own, oth)


def middle_kernel(where_ref, ctx_ref, *refs):
    pieces, refs = refs[:8], refs[8:]
    res_ref, router_ref, ids_ref, hidden_ref, out_ref, gate_ref, target_ref = refs[:7]
    halves, proj, res, sems = refs[7:]
    own, place = where_ref[0], (where_ref[1], where_ref[2])
    copies = [pltpu.make_async_copy(res_ref.at[0], res, sems.at[32])]
    for n in range(8):
        core = own if n < 4 else 1 - own
        for first in range(4):
            along = (place[0] + jnp.where(core == 0, first, n % 4)) % 4
            across = (place[1] + jnp.where(core == 0, n % 4, first)) % 4
            copies.append(
                pltpu.make_async_copy(
                    pieces[n].at[first], proj.at[core, along * 4 + across], sems.at[n * 4 + first]
                )
            )
    for copy in copies:
        copy.start()
    for h in range(HEADS):
        for c in range(2):
            halves[c * 64 : (c + 1) * 64, h * 128 : (h + 1) * 128] = ctx_ref[h * 2 + c]
    for copy in copies:
        copy.wait()
    attn = jnp.dot(halves[...], proj[...].reshape(1024, 1024), preferred_element_type=F32)
    hidden = (res[...].astype(F32) + attn).astype(BF)
    hidden_ref[...] = hidden
    wide = hidden.astype(F32)
    mean_square = jnp.mean(wide * wide, axis=1, keepdims=True)
    normed = (wide * lax.rsqrt(mean_square + 1e-06)).astype(BF)
    affinity = jax.nn.sigmoid(
        lax.dot_general(
            router_ref[...], normed, (((1,), (1,)), ((), ())), preferred_element_type=F32
        )
    )
    experts, tokens = affinity.shape
    expert = lax.broadcasted_iota(jnp.int32, (experts, tokens), 0)
    hot = [expert == ids_ref[k : k + 1, :] for k in range(TOP)]
    picked = [jnp.sum(jnp.where(m, affinity, 0.0), axis=0, keepdims=True) for m in hot]
    whole = picked[0] + picked[1]
    before = (
        lax.broadcasted_iota(jnp.int32, (tokens, tokens), 0)
        < lax.broadcasted_iota(jnp.int32, (tokens, tokens), 1)
    ).astype(F32).astype(BF)
    counts = jnp.zeros((experts, 1), F32)
    slot_row = lax.broadcasted_iota(jnp.int32, (experts * SLOT, tokens), 0)
    dispatch = jnp.zeros((experts * SLOT, tokens), F32)
    for k in range(TOP):
        one = hot[k].astype(F32)
        rank = jnp.dot(one.astype(BF), before, preferred_element_type=F32) + counts
        slot = jnp.sum(rank * one, axis=0, keepdims=True).astype(jnp.int32)
        counts = counts + jnp.sum(one, axis=1, keepdims=True)
        target = ids_ref[k : k + 1, :] * SLOT + slot
        dispatch = dispatch + (slot_row == target).astype(F32)
        gate_ref[k : k + 1, :] = picked[k] / whole
        target_ref[k : k + 1, :] = target
    out_ref[...] = jnp.dot(dispatch.astype(BF), normed, preferred_element_type=F32).astype(BF)


def middle(where, ctx, own, oth, residual, router, ids):
    tokens, width = residual.shape[1:]
    experts = router.shape[1]
    return pl.pallas_call(
        middle_kernel,
        out_shape=(
            jax.ShapeDtypeStruct((tokens, width), BF),
            jax.ShapeDtypeStruct((experts * SLOT, width), BF),
            jax.ShapeDtypeStruct((TOP, tokens), F32),
            jax.ShapeDtypeStruct((TOP, tokens), jnp.int32),
        ),
        in_specs=[SMEM, VMEM] + [ANY] * 9 + [VMEM, VMEM],
        out_specs=(VMEM,) * 4,
        scratch_shapes=[
            pltpu.VMEM((128, 1024), BF),
            pltpu.VMEM((2, 16, 32, 1024), BF),
            pltpu.VMEM((128, 1024), BF),
            pltpu.SemaphoreType.DMA((33,)),
        ],
        compiler_params=params(16),
        cost_estimate=pl.CostEstimate(
            flops=2 * 128 * 1024 * 1600, bytes_accessed=4 << 20, transcendentals=4096
        ),
    )(where, ctx, *own, *oth, residual, router.T, ids[0].T)


def pick_kernel(core_ref, weights_ref, after_ref, *refs):
    sems = refs[-1]
    core = core_ref[0]
    copies = [
        pltpu.make_async_copy(
            weights_ref.at[pl.ds((1 - core) * 8 + n * PART, PART)], ref, sems.at[n]
        )
        for n, ref in enumerate(refs[:-2])
    ]
    copies.append(
        pltpu.make_async_copy(weights_ref.at[pl.ds(core * 8, 8)], refs[-2], sems.at[8 // PART])
    )
    for copy in copies:
        copy.start()
    for copy in copies:
        copy.wait()


def pick(core, weights, after):
    parts = 8 // PART
    one = weights.shape[1:]
    return pl.pallas_call(
        pick_kernel,
        out_shape=(jax.ShapeDtypeStruct((PART,) + one, BF),) * parts
        + (jax.ShapeDtypeStruct((8,) + one, BF),),
        in_specs=[SMEM, HBM, ANY],
        out_specs=(ANY,) * (parts + 1),
        scratch_shapes=[pltpu.SemaphoreType.DMA((parts + 1,))],
        compiler_params=params(52),
        cost_estimate=pl.CostEstimate(flops=0, bytes_accessed=8 << 20, transcendentals=0),
    )(core, weights, after)


def expert_kernel(core_ref, x_ref, own_ref, *refs):
    oth_refs, (out_ref, up, down, sems) = refs[: 8 // PART], refs[8 // PART :]
    core = core_ref[0]
    pieces = [(own_ref, slice(0, 8), core)]
    pieces += [
        (ref, slice(n * PART, (n + 1) * PART), 1 - core) for n, ref in enumerate(oth_refs)
    ]
    early, late = [], []
    for source, z, place in pieces:
        early += [
            (source.at[:, 0:64, :], up.at[z, place, :, 0:1024]),
            (source.at[:, 64:96, 0:512], up.at[z, place, 0:32, 1024:1536]),
            (source.at[:, 64:96, 512:1024], up.at[z, place, 32:64, 1024:1536]),
        ]
        late.append((source.at[:, 96:144, :], down.at[z, place]))
    copies = [
        pltpu.make_async_copy(src, dst, sems.at[n]) for n, (src, dst) in enumerate(early + late)
    ]
    for copy in copies:
        copy.start()
    for copy in copies[: len(early)]:
        copy.wait()
    ff = down.shape[0] * 2 * down.shape[2]
    up_all = up[...].reshape(1024, 2 * ff)
    inner = jnp.dot(x_ref[...], up_all, preferred_element_type=F32)
    activation = (jax.nn.silu(inner[:, :ff]) * inner[:, ff:]).astype(BF)
    for copy in copies[len(early) :]:
        copy.wait()
    out_ref[...] = jnp.dot(
        activation, down[...].reshape(ff, 1024), preferred_element_type=F32
    ).astype(BF)


def experts(core, x, own, oth):
    rows = x.shape[0]
    return pl.pallas_call(
        expert_kernel,
        out_shape=jax.ShapeDtypeStruct((rows, 1024), BF),
        in_specs=[SMEM, VMEM, ANY] + [ANY] * len(oth),
        out_specs=VMEM,
        scratch_shapes=[
            pltpu.VMEM((8, 2, 64, 1536), BF),
            pltpu.VMEM((8, 2, 48, 1024), BF),
            pltpu.SemaphoreType.DMA((4 * (1 + len(oth)),)),
        ],
        compiler_params=params(24),
        cost_estimate=pl.CostEstimate(
            flops=2 * rows * 1024 * 2304, bytes_accessed=7 << 20, transcendentals=rows * 768
        ),
    )(core, x, own, *oth)


def combine_kernel(back_ref, hidden_ref, gate_ref, target_ref, out_ref):
    tokens = hidden_ref.shape[0]
    slot_row = lax.broadcasted_iota(jnp.int32, (back_ref.shape[0], tokens), 0)
    pad = jnp.zeros((8 - TOP, tokens), F32)
    gates = jnp.transpose(jnp.concatenate([gate_ref[...], pad], axis=0))
    total = hidden_ref[...].astype(F32)
    moe = None
    for k in range(TOP):
        choose = (slot_row == target_ref[k : k + 1, :]).astype(F32).astype(BF)
        pair = lax.dot_general(
            choose, back_ref[...], (((0,), (0,)), ((), ())), preferred_element_type=F32
        ) * gates[:, k : k + 1]
        moe = pair if moe is None else moe + pair
    out_ref[0] = (total + moe).astype(BF)


def combine(back, hidden, gate, target):
    return pl.pallas_call(
        combine_kernel,
        out_shape=jax.ShapeDtypeStruct((1,) + hidden.shape, BF),
        in_specs=[VMEM] * 4,
        out_specs=VMEM,
        compiler_params=params(16),
    )(back, hidden, gate, target)


def on_device(
    residual, query_rows, key_rows, value_rows, out_proj, router, expert_ids,
    expert_gate_up, expert_down,
):
    core_index = lax.axis_index("core")
    core = core_index.astype(jnp.int32).reshape(1)
    packed = copies_call(
        weights_plan, 4, jax.ShapeDtypeStruct((144, 1024), BF), expert_gate_up[0], expert_down[0]
    )
    weights = lax.all_gather(packed, ("zhi", "zlo"), axis=0, tiled=False)

    moved = lax.ppermute(out_proj, ALL, HALF_MOVE)
    shard = jnp.where(lax.axis_index("zhi") == core_index, out_proj, moved)
    line = jnp.stack([shard] + [lax.ppermute(shard, ALL, plane_pairs(0, d)) for d in (1, 2, 3)])
    proj_own = [line] + [lax.ppermute(line, ALL, plane_pairs(1, d)) for d in (1, 2, 3)]

    halves = (2, 64, 1024)
    heads = copies_call(
        heads_plan, 24, jax.ShapeDtypeStruct((8, 2, 192, 128), BF),
        query_rows.reshape(halves), key_rows.reshape(halves), value_rows.reshape(halves),
        order=(moved,),
    )
    heads = lax.all_to_all(
        heads.reshape(16, 192, 128), ("zlo", "core"), split_axis=0, concat_axis=0, tiled=True
    )
    keys = copies_call(
        keys_plan, 1, jax.ShapeDtypeStruct((16, 128, 128), BF), heads, order=tuple(proj_own),
        mib=2,
    )
    oth_keys = lax.ppermute(keys, ALL, CORE_SWAP)
    proj_oth = [lax.ppermute(p, ALL, CORE_SWAP) for p in proj_own]
    context = attention(core, heads, oth_keys)
    context = lax.all_to_all(context, ("zlo", "core"), split_axis=0, concat_axis=0, tiled=True)

    xy = lax.axis_index("xy").astype(jnp.int32).reshape(1)
    where = jnp.concatenate([core, xy // 4, xy % 4])
    hidden, outgoing, gate, target = middle(
        where, context, proj_own, proj_oth, residual, router, expert_ids
    )
    arrived = lax.all_to_all(
        outgoing.reshape(32, SLOT, 1024), ("core", "xy"), split_axis=0, concat_axis=0, tiled=True
    )
    *to_send, own_weights = pick(core, weights, target)
    oth_weights = [lax.ppermute(w, ALL, CORE_SWAP) for w in to_send]
    produced = experts(core, arrived.reshape(32 * SLOT, 1024), own_weights, oth_weights)
    back = lax.all_to_all(
        produced.reshape(32, SLOT, 1024), ("core", "xy"), split_axis=0, concat_axis=0, tiled=True
    )
    return combine(back.reshape(32 * SLOT, 1024), hidden, gate, target)


def solution(mesh):
    fine = Mesh(mesh.devices.reshape(8, 2, 2, 16), ALL)
    rows = P(("zhi", "xy"), ("zlo", "core"), None)
    return jax.shard_map(
        on_device,
        mesh=fine,
        in_specs=(rows, rows, rows, rows, P(("zhi", "xy"), None), P(), rows, rows, rows),
        out_specs=rows,
        check_vma=False,
    )
```

```python
import functools

import jax
import jax.numpy as jnp
from jax import lax
from jax.experimental import pallas as pl
from jax.experimental.pallas import tpu as pltpu
from jax.sharding import Mesh, PartitionSpec as P

HEADS = 8
HEAD_DIM = 128
TOP = 2
SLOT = 16
PART = 2
NEG_FILL = -1e30
LOG2E = 1.4426950408889634
BF = jnp.bfloat16
F32 = jnp.float32
ALL = ("zlo", "core", "zhi", "xy")

VMEM = pl.BlockSpec(memory_space=pltpu.VMEM)
SMEM = pl.BlockSpec(memory_space=pltpu.SMEM)
ANY = pl.BlockSpec(memory_space=pl.ANY)
HBM = pl.BlockSpec(memory_space=pltpu.HBM)


def linear(zlo, core, zhi, xy):
    return ((zlo * 2 + core) * 2 + zhi) * 16 + xy


def all_pairs(move):
    pairs = []
    for zlo in range(8):
        for core in range(2):
            for zhi in range(2):
                for xy in range(16):
                    target = move(zlo, core, zhi, xy)
                    if target is not None:
                        pairs.append((linear(zlo, core, zhi, xy), linear(*target)))
    return pairs


CORE_SWAP = all_pairs(lambda zlo, core, zhi, xy: (zlo, 1 - core, zhi, xy))
HALF_MOVE = all_pairs(lambda zlo, core, zhi, xy: (zlo, core, 1 - zhi, xy) if zhi == core else None)


def plane_pairs(phase, step):
    def move(zlo, core, zhi, xy):
        x, y = divmod(xy, 4)
        if (phase + core) % 2 == 0:
            x = (x - step) % 4
        else:
            y = (y - step) % 4
        return zlo, core, zhi, x * 4 + y

    return all_pairs(move)


def params(mib):
    return pltpu.CompilerParams(vmem_limit_bytes=mib << 20)


def pack_weights_kernel(up_ref, down_ref, out_ref, up, down, sems):
    copies = [
        pltpu.make_async_copy(up_ref.at[0], up, sems.at[0]),
        pltpu.make_async_copy(down_ref.at[0], down, sems.at[1]),
    ]
    for copy in copies:
        copy.start()
    for copy in copies:
        copy.wait()
    out_ref[0:64, :] = up[:, 0:1024]
    out_ref[64:96, 0:512] = up[0:32, 1024:1536]
    out_ref[64:96, 512:1024] = up[32:64, 1024:1536]
    out_ref[96:144, :] = down[...]


def pack_weights(gate_up, down):
    return pl.pallas_call(
        pack_weights_kernel,
        out_shape=jax.ShapeDtypeStruct((144, 1024), BF),
        in_specs=[HBM, HBM],
        out_specs=VMEM,
        scratch_shapes=[
            pltpu.VMEM(gate_up.shape[1:], BF),
            pltpu.VMEM(down.shape[1:], BF),
            pltpu.SemaphoreType.DMA((2,)),
        ],
        compiler_params=params(56),
    )(gate_up, down)


def pack_heads_kernel(q_ref, k_ref, v_ref, after_ref, out_ref, rows, sems):
    copies = [
        pltpu.make_async_copy(ref.at[0], rows.at[j], sems.at[j])
        for j, ref in enumerate((q_ref, k_ref, v_ref))
    ]
    for copy in copies:
        copy.start()
    for j, copy in enumerate(copies):
        copy.wait()
        for h in range(HEADS):
            for c in range(2):
                out_ref[h * 2 + c, j * 64 : (j + 1) * 64, :] = rows[
                    j, c * 64 : (c + 1) * 64, h * 128 : (h + 1) * 128
                ]


def pack_heads(q, k, v, after):
    return pl.pallas_call(
        pack_heads_kernel,
        out_shape=jax.ShapeDtypeStruct((16, 192, 128), BF),
        in_specs=[HBM] * 3 + [ANY],
        out_specs=VMEM,
        scratch_shapes=[pltpu.VMEM((3,) + q.shape[1:], BF), pltpu.SemaphoreType.DMA((3,))],
        compiler_params=params(56),
    )(q, k, v, after)


def keys_kernel(heads_ref, *refs):
    refs[-1][...] = heads_ref[:, 64:192, :]


def keys_of(heads, after):
    return pl.pallas_call(
        keys_kernel,
        out_shape=jax.ShapeDtypeStruct((16, 128, 128), BF),
        in_specs=[VMEM] + [ANY] * len(after),
        out_specs=VMEM,
        compiler_params=params(4),
    )(heads, *after)


def attention_kernel(core_ref, own_ref, oth_ref, out_ref):
    core = core_ref[0]
    queries = own_ref[:, 0:64, :].reshape(1024, 128)
    own_keys = own_ref[:, 64:128, :].reshape(1024, 128)
    own_values = own_ref[:, 128:192, :].reshape(1024, 128)
    oth_keys = oth_ref[:, 0:64, :].reshape(1024, 128)
    oth_values = oth_ref[:, 64:128, :].reshape(1024, 128)
    scale = (HEAD_DIM ** (-0.5)) * LOG2E
    rows = 256
    row = lax.broadcasted_iota(jnp.int32, (rows, rows), 0)
    col = lax.broadcasted_iota(jnp.int32, (rows, rows), 1)
    own_allowed = col <= row
    oth_allowed = (col // 64) < (row // 64) + core
    contract = (((1,), (1,)), ((), ()))
    for j in range(1024 // rows):
        q = queries[j * rows : (j + 1) * rows]
        n = j * rows
        pieces = []
        for keys, values, allowed in (
            (own_keys, own_values, own_allowed),
            (oth_keys, oth_values, oth_allowed),
        ):
            if n:
                s = lax.dot_general(q, keys[:n], contract, preferred_element_type=F32) * scale
                pieces.append((s, values[:n]))
            s = lax.dot_general(q, keys[n : n + rows], contract, preferred_element_type=F32) * scale
            pieces.append((jnp.where(allowed, s, NEG_FILL), values[n : n + rows]))
        top = functools.reduce(jnp.maximum, [jnp.max(s, axis=1, keepdims=True) for s, _ in pieces])
        acc = jnp.zeros((rows, HEAD_DIM), F32)
        total = jnp.zeros((rows, 1), F32)
        for s, values in pieces:
            e = jnp.exp2(s - top)
            total = total + jnp.sum(e, axis=1, keepdims=True)
            acc = acc + jnp.dot(e.astype(BF), values, preferred_element_type=F32)
        out_ref[j * (rows // 64) : (j + 1) * (rows // 64)] = (
            (acc / total).astype(BF).reshape(rows // 64, 64, HEAD_DIM)
        )


def attention(core, own, oth):
    return pl.pallas_call(
        attention_kernel,
        out_shape=jax.ShapeDtypeStruct((16, 64, 128), BF),
        in_specs=[SMEM, VMEM, VMEM],
        out_specs=VMEM,
        compiler_params=params(20),
        cost_estimate=pl.CostEstimate(
            flops=2 * 2 * 1024 * 1280 * 128, bytes_accessed=2 << 20, transcendentals=1024 * 1280
        ),
    )(core, own, oth)


def middle_kernel(where_ref, ctx_ref, *refs):
    pieces, refs = refs[:8], refs[8:]
    res_ref, router_ref, ids_ref, hidden_ref, out_ref, gate_ref, target_ref = refs[:7]
    halves, proj = refs[7:]
    own, place = where_ref[0], (where_ref[1], where_ref[2])
    for n in range(8):
        core = own if n < 4 else 1 - own
        for first in range(4):
            along = (place[0] + jnp.where(core == 0, first, n % 4)) % 4
            across = (place[1] + jnp.where(core == 0, n % 4, first)) % 4
            proj[core, along * 4 + across] = pieces[n][first]
    for h in range(HEADS):
        for c in range(2):
            halves[c * 64 : (c + 1) * 64, h * 128 : (h + 1) * 128] = ctx_ref[h * 2 + c]
    attn = jnp.dot(halves[...], proj[...].reshape(1024, 1024), preferred_element_type=F32)
    hidden = (res_ref[0].astype(F32) + attn).astype(BF)
    hidden_ref[...] = hidden
    wide = hidden.astype(F32)
    mean_square = jnp.mean(wide * wide, axis=1, keepdims=True)
    normed = (wide * lax.rsqrt(mean_square + 1e-06)).astype(BF)
    affinity = jax.nn.sigmoid(
        lax.dot_general(
            router_ref[...], normed, (((1,), (1,)), ((), ())), preferred_element_type=F32
        )
    )
    experts, tokens = affinity.shape
    expert = lax.broadcasted_iota(jnp.int32, (experts, tokens), 0)
    hot = [expert == ids_ref[k : k + 1, :] for k in range(TOP)]
    picked = [jnp.sum(jnp.where(m, affinity, 0.0), axis=0, keepdims=True) for m in hot]
    whole = picked[0] + picked[1]
    before = (
        lax.broadcasted_iota(jnp.int32, (tokens, tokens), 0)
        < lax.broadcasted_iota(jnp.int32, (tokens, tokens), 1)
    ).astype(F32).astype(BF)
    counts = jnp.zeros((experts, 1), F32)
    slot_row = lax.broadcasted_iota(jnp.int32, (experts * SLOT, tokens), 0)
    dispatch = jnp.zeros((experts * SLOT, tokens), F32)
    for k in range(TOP):
        one = hot[k].astype(F32)
        rank = jnp.dot(one.astype(BF), before, preferred_element_type=F32) + counts
        slot = jnp.sum(rank * one, axis=0, keepdims=True).astype(jnp.int32)
        counts = counts + jnp.sum(one, axis=1, keepdims=True)
        target = ids_ref[k : k + 1, :] * SLOT + slot
        dispatch = dispatch + (slot_row == target).astype(F32)
        gate_ref[k : k + 1, :] = picked[k] / whole
        target_ref[k : k + 1, :] = target
    out_ref[...] = jnp.dot(dispatch.astype(BF), normed, preferred_element_type=F32).astype(BF)


def middle(where, ctx, own, oth, residual, router, ids):
    tokens, width = residual.shape[1:]
    experts = router.shape[1]
    return pl.pallas_call(
        middle_kernel,
        out_shape=(
            jax.ShapeDtypeStruct((tokens, width), BF),
            jax.ShapeDtypeStruct((experts * SLOT, width), BF),
            jax.ShapeDtypeStruct((TOP, tokens), F32),
            jax.ShapeDtypeStruct((TOP, tokens), jnp.int32),
        ),
        in_specs=[SMEM] + [VMEM] * 12,
        out_specs=(VMEM,) * 4,
        scratch_shapes=[
            pltpu.VMEM((128, 1024), BF),
            pltpu.VMEM((2, 16, 32, 1024), BF),
        ],
        compiler_params=params(16),
        cost_estimate=pl.CostEstimate(
            flops=2 * 128 * 1024 * 1600, bytes_accessed=4 << 20, transcendentals=4096
        ),
    )(where, ctx, *own, *oth, residual, router.T, ids[0].T)


def pick_kernel(core_ref, weights_ref, after_ref, *refs):
    sems = refs[-1]
    core = core_ref[0]
    copies = [
        pltpu.make_async_copy(
            weights_ref.at[pl.ds((1 - core) * 8 + n * PART, PART)], ref, sems.at[n]
        )
        for n, ref in enumerate(refs[:-2])
    ]
    copies.append(
        pltpu.make_async_copy(weights_ref.at[pl.ds(core * 8, 8)], refs[-2], sems.at[8 // PART])
    )
    for copy in copies:
        copy.start()
    for copy in copies:
        copy.wait()


def pick(core, weights, after):
    parts = 8 // PART
    one = weights.shape[1:]
    return pl.pallas_call(
        pick_kernel,
        out_shape=(jax.ShapeDtypeStruct((PART,) + one, BF),) * parts
        + (jax.ShapeDtypeStruct((8,) + one, BF),),
        in_specs=[SMEM, HBM, ANY],
        out_specs=(VMEM,) * (parts + 1),
        scratch_shapes=[pltpu.SemaphoreType.DMA((parts + 1,))],
        compiler_params=params(52),
        cost_estimate=pl.CostEstimate(flops=0, bytes_accessed=8 << 20, transcendentals=0),
    )(core, weights, after)


def expert_kernel(core_ref, x_ref, own_ref, *refs):
    oth_refs, (out_ref, up, down) = refs[: 8 // PART], refs[8 // PART :]
    core = core_ref[0]
    pieces = [(own_ref, slice(0, 8), core)]
    pieces += [
        (ref, slice(n * PART, (n + 1) * PART), 1 - core) for n, ref in enumerate(oth_refs)
    ]
    for source, z, place in pieces:
        up[z, place, :, 0:1024] = source[:, 0:64, :]
        up[z, place, 0:32, 1024:1536] = source[:, 64:96, 0:512]
        up[z, place, 32:64, 1024:1536] = source[:, 64:96, 512:1024]
        down[z, place] = source[:, 96:144, :]
    ff = down.shape[0] * 2 * down.shape[2]
    inner = jnp.dot(x_ref[...], up[...].reshape(1024, 2 * ff), preferred_element_type=F32)
    activation = (jax.nn.silu(inner[:, :ff]) * inner[:, ff:]).astype(BF)
    out_ref[...] = jnp.dot(
        activation, down[...].reshape(ff, 1024), preferred_element_type=F32
    ).astype(BF)


def experts(core, x, own, oth):
    rows = x.shape[0]
    return pl.pallas_call(
        expert_kernel,
        out_shape=jax.ShapeDtypeStruct((rows, 1024), BF),
        in_specs=[SMEM, VMEM, VMEM] + [VMEM] * len(oth),
        out_specs=VMEM,
        scratch_shapes=[
            pltpu.VMEM((8, 2, 64, 1536), BF),
            pltpu.VMEM((8, 2, 48, 1024), BF),
        ],
        compiler_params=params(24),
        cost_estimate=pl.CostEstimate(
            flops=2 * rows * 1024 * 2304, bytes_accessed=7 << 20, transcendentals=rows * 768
        ),
    )(core, x, own, *oth)


def combine_kernel(back_ref, hidden_ref, gate_ref, target_ref, out_ref):
    tokens = hidden_ref.shape[0]
    slot_row = lax.broadcasted_iota(jnp.int32, (back_ref.shape[0], tokens), 0)
    pad = jnp.zeros((8 - TOP, tokens), F32)
    gates = jnp.transpose(jnp.concatenate([gate_ref[...], pad], axis=0))
    total = hidden_ref[...].astype(F32)
    moe = None
    for k in range(TOP):
        choose = (slot_row == target_ref[k : k + 1, :]).astype(F32).astype(BF)
        pair = lax.dot_general(
            choose, back_ref[...], (((0,), (0,)), ((), ())), preferred_element_type=F32
        ) * gates[:, k : k + 1]
        moe = pair if moe is None else moe + pair
    out_ref[0] = (total + moe).astype(BF)


def combine(back, hidden, gate, target):
    return pl.pallas_call(
        combine_kernel,
        out_shape=jax.ShapeDtypeStruct((1,) + hidden.shape, BF),
        in_specs=[VMEM] * 4,
        out_specs=VMEM,
        compiler_params=params(16),
    )(back, hidden, gate, target)


def on_device(
    residual, query_rows, key_rows, value_rows, out_proj, router, expert_ids,
    expert_gate_up, expert_down,
):
    core_index = lax.axis_index("core")
    core = core_index.astype(jnp.int32).reshape(1)
    packed = pack_weights(expert_gate_up, expert_down)
    weights = lax.all_gather(packed, ("zhi", "zlo"), axis=0, tiled=False)

    moved = lax.ppermute(out_proj, ALL, HALF_MOVE)
    shard = jnp.where(lax.axis_index("zhi") == core_index, out_proj, moved)
    line = jnp.stack([shard] + [lax.ppermute(shard, ALL, plane_pairs(0, d)) for d in (1, 2, 3)])
    proj_own = [line] + [lax.ppermute(line, ALL, plane_pairs(1, d)) for d in (1, 2, 3)]

    heads = pack_heads(query_rows, key_rows, value_rows, moved)
    heads = lax.all_to_all(heads, ("zlo", "core"), split_axis=0, concat_axis=0, tiled=True)
    keys = keys_of(heads, proj_own)
    oth_keys = lax.ppermute(keys, ALL, CORE_SWAP)
    proj_oth = [lax.ppermute(p, ALL, CORE_SWAP) for p in proj_own]
    context = attention(core, heads, oth_keys)
    context = lax.all_to_all(context, ("zlo", "core"), split_axis=0, concat_axis=0, tiled=True)

    xy = lax.axis_index("xy").astype(jnp.int32).reshape(1)
    where = jnp.concatenate([core, xy // 4, xy % 4])
    hidden, outgoing, gate, target = middle(
        where, context, proj_own, proj_oth, residual, router, expert_ids
    )
    arrived = lax.all_to_all(
        outgoing.reshape(32, SLOT, 1024), ("core", "xy"), split_axis=0, concat_axis=0, tiled=True
    )
    *to_send, own_weights = pick(core, weights, target)
    oth_weights = [lax.ppermute(w, ALL, CORE_SWAP) for w in to_send]
    produced = experts(core, arrived.reshape(32 * SLOT, 1024), own_weights, oth_weights)
    back = lax.all_to_all(
        produced.reshape(32, SLOT, 1024), ("core", "xy"), split_axis=0, concat_axis=0, tiled=True
    )
    return combine(back.reshape(32 * SLOT, 1024), hidden, gate, target)


def solution(mesh):
    fine = Mesh(mesh.devices.reshape(8, 2, 2, 16), ALL)
    rows = P(("zhi", "xy"), ("zlo", "core"), None)
    return jax.shard_map(
        on_device,
        mesh=fine,
        in_specs=(rows, rows, rows, rows, P(("zhi", "xy"), None), P(), rows, rows, rows),
        out_specs=rows,
        check_vma=False,
    )
```

```python
import functools

import jax
import jax.numpy as jnp
from jax import lax
from jax.experimental import pallas as pl
from jax.experimental.pallas import tpu as pltpu
from jax.sharding import Mesh, PartitionSpec as P

HEADS = 8
HEAD_DIM = 128
TOP = 2
SLOT = 16
PART = 2
NEG_FILL = -1e30
LOG2E = 1.4426950408889634
BF = jnp.bfloat16
F32 = jnp.float32
ALL = ("zlo", "core", "zhi", "xy")

VMEM = pl.BlockSpec(memory_space=pltpu.VMEM)
SMEM = pl.BlockSpec(memory_space=pltpu.SMEM)
ANY = pl.BlockSpec(memory_space=pl.ANY)
HBM = pl.BlockSpec(memory_space=pltpu.HBM)


def linear(zlo, core, zhi, xy):
    return ((zlo * 2 + core) * 2 + zhi) * 16 + xy


def all_pairs(move):
    pairs = []
    for zlo in range(8):
        for core in range(2):
            for zhi in range(2):
                for xy in range(16):
                    target = move(zlo, core, zhi, xy)
                    if target is not None:
                        pairs.append((linear(zlo, core, zhi, xy), linear(*target)))
    return pairs


CORE_SWAP = all_pairs(lambda zlo, core, zhi, xy: (zlo, 1 - core, zhi, xy))
HALF_MOVE = all_pairs(lambda zlo, core, zhi, xy: (zlo, core, 1 - zhi, xy) if zhi == core else None)


def plane_pairs(phase, step):
    def move(zlo, core, zhi, xy):
        x, y = divmod(xy, 4)
        if (phase + core) % 2 == 0:
            x = (x - step) % 4
        else:
            y = (y - step) % 4
        return zlo, core, zhi, x * 4 + y

    return all_pairs(move)


def params(mib):
    return pltpu.CompilerParams(vmem_limit_bytes=mib << 20)


def pack_weights_kernel(up_ref, down_ref, out_ref, up, down, sems):
    copies = [
        pltpu.make_async_copy(up_ref.at[0], up, sems.at[0]),
        pltpu.make_async_copy(down_ref.at[0], down, sems.at[1]),
    ]
    for copy in copies:
        copy.start()
    for copy in copies:
        copy.wait()
    out_ref[0:64, :] = up[:, 0:1024]
    out_ref[64:96, 0:512] = up[0:32, 1024:1536]
    out_ref[64:96, 512:1024] = up[32:64, 1024:1536]
    out_ref[96:144, :] = down[...]


def pack_weights(gate_up, down):
    return pl.pallas_call(
        pack_weights_kernel,
        out_shape=jax.ShapeDtypeStruct((144, 1024), BF),
        in_specs=[HBM, HBM],
        out_specs=VMEM,
        scratch_shapes=[
            pltpu.VMEM(gate_up.shape[1:], BF),
            pltpu.VMEM(down.shape[1:], BF),
            pltpu.SemaphoreType.DMA((2,)),
        ],
        compiler_params=params(56),
    )(gate_up, down)


def pack_heads_kernel(q_ref, k_ref, v_ref, out_ref, rows, sems):
    copies = [
        pltpu.make_async_copy(ref.at[0], rows.at[j], sems.at[j])
        for j, ref in enumerate((q_ref, k_ref, v_ref))
    ]
    for copy in copies:
        copy.start()
    for j, copy in enumerate(copies):
        copy.wait()
        for h in range(HEADS):
            for c in range(2):
                out_ref[h * 2 + c, j * 64 : (j + 1) * 64, :] = rows[
                    j, c * 64 : (c + 1) * 64, h * 128 : (h + 1) * 128
                ]


def pack_heads(q, k, v):
    return pl.pallas_call(
        pack_heads_kernel,
        out_shape=jax.ShapeDtypeStruct((16, 192, 128), BF),
        in_specs=[HBM] * 3,
        out_specs=VMEM,
        scratch_shapes=[pltpu.VMEM((3,) + q.shape[1:], BF), pltpu.SemaphoreType.DMA((3,))],
        compiler_params=params(56),
        cost_estimate=pl.CostEstimate(flops=0, bytes_accessed=20 << 20, transcendentals=0),
    )(q, k, v)


def keys_kernel(heads_ref, *refs):
    refs[-1][...] = heads_ref[:, 64:192, :]


def keys_of(heads, after):
    return pl.pallas_call(
        keys_kernel,
        out_shape=jax.ShapeDtypeStruct((16, 128, 128), BF),
        in_specs=[VMEM] + [ANY] * len(after),
        out_specs=VMEM,
        compiler_params=params(4),
    )(heads, *after)


def line_kernel(*refs):
    for n, ref in enumerate(refs[:4]):
        refs[-1][n] = ref[...]


def line_of(pieces, after):
    return pl.pallas_call(
        line_kernel,
        out_shape=jax.ShapeDtypeStruct((4,) + pieces[0].shape, BF),
        in_specs=[VMEM] * 4 + [ANY],
        out_specs=VMEM,
        compiler_params=params(4),
    )(*pieces, after)


def attention_kernel(core_ref, own_ref, oth_ref, out_ref):
    core = core_ref[0]
    queries = own_ref[:, 0:64, :].reshape(1024, 128)
    own_keys = own_ref[:, 64:128, :].reshape(1024, 128)
    own_values = own_ref[:, 128:192, :].reshape(1024, 128)
    oth_keys = oth_ref[:, 0:64, :].reshape(1024, 128)
    oth_values = oth_ref[:, 64:128, :].reshape(1024, 128)
    scale = (HEAD_DIM ** (-0.5)) * LOG2E
    rows = 256
    row = lax.broadcasted_iota(jnp.int32, (rows, rows), 0)
    col = lax.broadcasted_iota(jnp.int32, (rows, rows), 1)
    own_allowed = col <= row
    oth_allowed = (col // 64) < (row // 64) + core
    contract = (((1,), (1,)), ((), ()))
    for j in range(1024 // rows):
        q = queries[j * rows : (j + 1) * rows]
        n = j * rows
        pieces = []
        for keys, values, allowed in (
            (own_keys, own_values, own_allowed),
            (oth_keys, oth_values, oth_allowed),
        ):
            if n:
                s = lax.dot_general(q, keys[:n], contract, preferred_element_type=F32) * scale
                pieces.append((s, values[:n]))
            s = lax.dot_general(q, keys[n : n + rows], contract, preferred_element_type=F32) * scale
            pieces.append((jnp.where(allowed, s, NEG_FILL), values[n : n + rows]))
        top = functools.reduce(jnp.maximum, [jnp.max(s, axis=1, keepdims=True) for s, _ in pieces])
        acc = jnp.zeros((rows, HEAD_DIM), F32)
        total = jnp.zeros((rows, 1), F32)
        for s, values in pieces:
            e = jnp.exp2(s - top)
            total = total + jnp.sum(e, axis=1, keepdims=True)
            acc = acc + jnp.dot(e.astype(BF), values, preferred_element_type=F32)
        out_ref[j * (rows // 64) : (j + 1) * (rows // 64)] = (
            (acc / total).astype(BF).reshape(rows // 64, 64, HEAD_DIM)
        )


def attention(core, own, oth):
    return pl.pallas_call(
        attention_kernel,
        out_shape=jax.ShapeDtypeStruct((16, 64, 128), BF),
        in_specs=[SMEM, VMEM, VMEM],
        out_specs=VMEM,
        compiler_params=params(20),
        cost_estimate=pl.CostEstimate(
            flops=2 * 2 * 1024 * 1280 * 128, bytes_accessed=2 << 20, transcendentals=1024 * 1280
        ),
    )(core, own, oth)


def middle_kernel(where_ref, ctx_ref, *refs):
    pieces, refs = refs[:8], refs[8:]
    res_ref, router_ref, ids_ref, hidden_ref, out_ref, gate_ref, target_ref = refs[:7]
    halves, proj = refs[7:]
    own, place = where_ref[0], (where_ref[1], where_ref[2])
    for n in range(8):
        core = own if n < 4 else 1 - own
        for first in range(4):
            along = (place[0] + jnp.where(core == 0, first, n % 4)) % 4
            across = (place[1] + jnp.where(core == 0, n % 4, first)) % 4
            proj[core, along * 4 + across] = pieces[n][first]
    for h in range(HEADS):
        for c in range(2):
            halves[c * 64 : (c + 1) * 64, h * 128 : (h + 1) * 128] = ctx_ref[h * 2 + c]
    attn = jnp.dot(halves[...], proj[...].reshape(1024, 1024), preferred_element_type=F32)
    hidden = (res_ref[0].astype(F32) + attn).astype(BF)
    hidden_ref[...] = hidden
    wide = hidden.astype(F32)
    mean_square = jnp.mean(wide * wide, axis=1, keepdims=True)
    normed = (wide * lax.rsqrt(mean_square + 1e-06)).astype(BF)
    affinity = jax.nn.sigmoid(
        lax.dot_general(
            router_ref[...], normed, (((1,), (1,)), ((), ())), preferred_element_type=F32
        )
    )
    experts, tokens = affinity.shape
    expert = lax.broadcasted_iota(jnp.int32, (experts, tokens), 0)
    hot = [expert == ids_ref[k : k + 1, :] for k in range(TOP)]
    picked = [jnp.sum(jnp.where(m, affinity, 0.0), axis=0, keepdims=True) for m in hot]
    whole = picked[0] + picked[1]
    before = (
        lax.broadcasted_iota(jnp.int32, (tokens, tokens), 0)
        < lax.broadcasted_iota(jnp.int32, (tokens, tokens), 1)
    ).astype(F32).astype(BF)
    counts = jnp.zeros((experts, 1), F32)
    slot_row = lax.broadcasted_iota(jnp.int32, (experts * SLOT, tokens), 0)
    dispatch = jnp.zeros((experts * SLOT, tokens), F32)
    for k in range(TOP):
        one = hot[k].astype(F32)
        rank = jnp.dot(one.astype(BF), before, preferred_element_type=F32) + counts
        slot = jnp.sum(rank * one, axis=0, keepdims=True).astype(jnp.int32)
        counts = counts + jnp.sum(one, axis=1, keepdims=True)
        target = ids_ref[k : k + 1, :] * SLOT + slot
        dispatch = dispatch + (slot_row == target).astype(F32)
        gate_ref[k : k + 1, :] = picked[k] / whole
        target_ref[k : k + 1, :] = target
    out_ref[...] = jnp.dot(dispatch.astype(BF), normed, preferred_element_type=F32).astype(BF)


def middle(where, ctx, own, oth, residual, router, ids):
    tokens, width = residual.shape[1:]
    experts = router.shape[1]
    return pl.pallas_call(
        middle_kernel,
        out_shape=(
            jax.ShapeDtypeStruct((tokens, width), BF),
            jax.ShapeDtypeStruct((experts * SLOT, width), BF),
            jax.ShapeDtypeStruct((TOP, tokens), F32),
            jax.ShapeDtypeStruct((TOP, tokens), jnp.int32),
        ),
        in_specs=[SMEM] + [VMEM] * 12,
        out_specs=(VMEM,) * 4,
        scratch_shapes=[
            pltpu.VMEM((128, 1024), BF),
            pltpu.VMEM((2, 16, 32, 1024), BF),
        ],
        compiler_params=params(16),
        cost_estimate=pl.CostEstimate(
            flops=2 * 128 * 1024 * 1600, bytes_accessed=4 << 20, transcendentals=4096
        ),
    )(where, ctx, *own, *oth, residual, router.T, ids[0].T)


def pick_kernel(flip, core_ref, weights_ref, after_ref, *refs):
    sems = refs[-1]
    core = core_ref[0]
    first = ((1 - core) if flip else core) * 8
    copies = []
    for n, ref in enumerate(refs[:-1]):
        size = ref.shape[0]
        copies.append(
            pltpu.make_async_copy(weights_ref.at[pl.ds(first + n * size, size)], ref, sems.at[n])
        )
    for copy in copies:
        copy.start()
    for copy in copies:
        copy.wait()


def pick(core, weights, after, flip, parts):
    return pl.pallas_call(
        functools.partial(pick_kernel, flip),
        out_shape=(jax.ShapeDtypeStruct((8 // parts,) + weights.shape[1:], BF),) * parts,
        in_specs=[SMEM, HBM, ANY],
        out_specs=(VMEM,) * parts,
        scratch_shapes=[pltpu.SemaphoreType.DMA((parts,))],
        compiler_params=params(52 if flip else 40),
        cost_estimate=pl.CostEstimate(flops=0, bytes_accessed=8 << 20, transcendentals=0),
    )(core, weights, after)


def expert_kernel(core_ref, x_ref, own_ref, *refs):
    oth_refs, (out_ref, up, down) = refs[: 8 // PART], refs[8 // PART :]
    core = core_ref[0]
    pieces = [(own_ref, slice(0, 8), core)]
    pieces += [
        (ref, slice(n * PART, (n + 1) * PART), 1 - core) for n, ref in enumerate(oth_refs)
    ]
    for source, z, place in pieces:
        up[z, place, :, 0:1024] = source[:, 0:64, :]
        up[z, place, 0:32, 1024:1536] = source[:, 64:96, 0:512]
        up[z, place, 32:64, 1024:1536] = source[:, 64:96, 512:1024]
        down[z, place] = source[:, 96:144, :]
    ff = down.shape[0] * 2 * down.shape[2]
    inner = jnp.dot(x_ref[...], up[...].reshape(1024, 2 * ff), preferred_element_type=F32)
    activation = (jax.nn.silu(inner[:, :ff]) * inner[:, ff:]).astype(BF)
    out_ref[...] = jnp.dot(
        activation, down[...].reshape(ff, 1024), preferred_element_type=F32
    ).astype(BF)


def experts(core, x, own, oth):
    rows = x.shape[0]
    return pl.pallas_call(
        expert_kernel,
        out_shape=jax.ShapeDtypeStruct((rows, 1024), BF),
        in_specs=[SMEM, VMEM, VMEM] + [VMEM] * len(oth),
        out_specs=VMEM,
        scratch_shapes=[
            pltpu.VMEM((8, 2, 64, 1536), BF),
            pltpu.VMEM((8, 2, 48, 1024), BF),
        ],
        compiler_params=params(24),
        cost_estimate=pl.CostEstimate(
            flops=2 * rows * 1024 * 2304, bytes_accessed=7 << 20, transcendentals=rows * 768
        ),
    )(core, x, own, *oth)


def combine_kernel(back_ref, hidden_ref, gate_ref, target_ref, out_ref):
    tokens = hidden_ref.shape[0]
    slot_row = lax.broadcasted_iota(jnp.int32, (back_ref.shape[0], tokens), 0)
    pad = jnp.zeros((8 - TOP, tokens), F32)
    gates = jnp.transpose(jnp.concatenate([gate_ref[...], pad], axis=0))
    total = hidden_ref[...].astype(F32)
    moe = None
    for k in range(TOP):
        choose = (slot_row == target_ref[k : k + 1, :]).astype(F32).astype(BF)
        pair = lax.dot_general(
            choose, back_ref[...], (((0,), (0,)), ((), ())), preferred_element_type=F32
        ) * gates[:, k : k + 1]
        moe = pair if moe is None else moe + pair
    out_ref[0] = (total + moe).astype(BF)


def combine(back, hidden, gate, target):
    return pl.pallas_call(
        combine_kernel,
        out_shape=jax.ShapeDtypeStruct((1,) + hidden.shape, BF),
        in_specs=[VMEM] * 4,
        out_specs=VMEM,
        compiler_params=params(16),
    )(back, hidden, gate, target)


def on_device(
    residual, query_rows, key_rows, value_rows, out_proj, router, expert_ids,
    expert_gate_up, expert_down,
):
    core_index = lax.axis_index("core")
    core = core_index.astype(jnp.int32).reshape(1)
    packed = pack_weights(expert_gate_up, expert_down)
    weights = lax.all_gather(packed, ("zhi", "zlo"), axis=0, tiled=False)

    moved = lax.ppermute(out_proj, ALL, HALF_MOVE)
    shard = jnp.where(lax.axis_index("zhi") == core_index, out_proj, moved)
    pieces = [shard] + [lax.ppermute(shard, ALL, plane_pairs(0, d)) for d in (1, 2, 3)]

    heads = pack_heads(query_rows, key_rows, value_rows)
    heads = lax.all_to_all(heads, ("zlo", "core"), split_axis=0, concat_axis=0, tiled=True)
    oth_keys = lax.ppermute(keys_of(heads, pieces), ALL, CORE_SWAP)
    context = attention(core, heads, oth_keys)

    line = line_of(pieces, context)
    proj_own = [line] + [lax.ppermute(line, ALL, plane_pairs(1, d)) for d in (1, 2, 3)]
    proj_oth = [lax.ppermute(p, ALL, CORE_SWAP) for p in proj_own]
    context = lax.all_to_all(context, ("zlo", "core"), split_axis=0, concat_axis=0, tiled=True)

    xy = lax.axis_index("xy").astype(jnp.int32).reshape(1)
    where = jnp.concatenate([core, xy // 4, xy % 4])
    hidden, outgoing, gate, target = middle(
        where, context, proj_own, proj_oth, residual, router, expert_ids
    )
    arrived = lax.all_to_all(
        outgoing.reshape(32, SLOT, 1024), ("core", "xy"), split_axis=0, concat_axis=0, tiled=True
    )
    to_send = pick(core, weights, target, True, 8 // PART)
    oth_weights = [lax.ppermute(w, ALL, CORE_SWAP) for w in to_send]
    (own_weights,) = pick(core, weights, target, False, 1)
    produced = experts(core, arrived.reshape(32 * SLOT, 1024), own_weights, oth_weights)
    back = lax.all_to_all(
        produced.reshape(32, SLOT, 1024), ("core", "xy"), split_axis=0, concat_axis=0, tiled=True
    )
    return combine(back.reshape(32 * SLOT, 1024), hidden, gate, target)


def solution(mesh):
    fine = Mesh(mesh.devices.reshape(8, 2, 2, 16), ALL)
    rows = P(("zhi", "xy"), ("zlo", "core"), None)
    return jax.shard_map(
        on_device,
        mesh=fine,
        in_specs=(rows, rows, rows, rows, P(("zhi", "xy"), None), P(), rows, rows, rows),
        out_specs=rows,
        check_vma=False,
    )
```

```python
import functools

import jax
import jax.numpy as jnp
from jax import lax
from jax.experimental import pallas as pl
from jax.experimental.pallas import tpu as pltpu
from jax.sharding import Mesh, PartitionSpec as P

HEADS = 8
HEAD_DIM = 128
TOP = 2
SLOT = 16
PARTS = (3, 3, 2)
NEG_FILL = -1e30
LOG2E = 1.4426950408889634
BF = jnp.bfloat16
F32 = jnp.float32
ALL = ("zlo", "core", "zhi", "xy")

VMEM = pl.BlockSpec(memory_space=pltpu.VMEM)
SMEM = pl.BlockSpec(memory_space=pltpu.SMEM)
ANY = pl.BlockSpec(memory_space=pl.ANY)
HBM = pl.BlockSpec(memory_space=pltpu.HBM)


def linear(zlo, core, zhi, xy):
    return ((zlo * 2 + core) * 2 + zhi) * 16 + xy


def all_pairs(move):
    pairs = []
    for zlo in range(8):
        for core in range(2):
            for zhi in range(2):
                for xy in range(16):
                    target = move(zlo, core, zhi, xy)
                    if target is not None:
                        pairs.append((linear(zlo, core, zhi, xy), linear(*target)))
    return pairs


CORE_SWAP = all_pairs(lambda zlo, core, zhi, xy: (zlo, 1 - core, zhi, xy))
HALF_MOVE = all_pairs(lambda zlo, core, zhi, xy: (zlo, core, 1 - zhi, xy) if zhi == core else None)


def plane_pairs(phase, step):
    def move(zlo, core, zhi, xy):
        x, y = divmod(xy, 4)
        if (phase + core) % 2 == 0:
            x = (x - step) % 4
        else:
            y = (y - step) % 4
        return zlo, core, zhi, x * 4 + y

    return all_pairs(move)


def params(mib):
    return pltpu.CompilerParams(vmem_limit_bytes=mib << 20)


def pack_weights_kernel(up_ref, down_ref, out_ref, up, down, sems):
    copies = [
        pltpu.make_async_copy(up_ref.at[0], up, sems.at[0]),
        pltpu.make_async_copy(down_ref.at[0], down, sems.at[1]),
    ]
    for copy in copies:
        copy.start()
    for copy in copies:
        copy.wait()
    out_ref[0:64, :] = up[:, 0:1024]
    out_ref[64:96, 0:512] = up[0:32, 1024:1536]
    out_ref[64:96, 512:1024] = up[32:64, 1024:1536]
    out_ref[96:144, :] = down[...]


def pack_weights(gate_up, down):
    return pl.pallas_call(
        pack_weights_kernel,
        out_shape=jax.ShapeDtypeStruct((144, 1024), BF),
        in_specs=[HBM, HBM],
        out_specs=VMEM,
        scratch_shapes=[
            pltpu.VMEM(gate_up.shape[1:], BF),
            pltpu.VMEM(down.shape[1:], BF),
            pltpu.SemaphoreType.DMA((2,)),
        ],
        compiler_params=params(56),
    )(gate_up, down)


def pack_heads_kernel(q_ref, k_ref, v_ref, after_ref, out_ref, rows, sems):
    copies = [
        pltpu.make_async_copy(ref.at[0], rows.at[j], sems.at[j])
        for j, ref in enumerate((q_ref, k_ref, v_ref))
    ]
    for copy in copies:
        copy.start()
    for j, copy in enumerate(copies):
        copy.wait()
        for h in range(HEADS):
            for c in range(2):
                out_ref[h * 2 + c, j * 64 : (j + 1) * 64, :] = rows[
                    j, c * 64 : (c + 1) * 64, h * 128 : (h + 1) * 128
                ]


def pack_heads(q, k, v, after):
    return pl.pallas_call(
        pack_heads_kernel,
        out_shape=jax.ShapeDtypeStruct((16, 192, 128), BF),
        in_specs=[HBM] * 3 + [ANY],
        out_specs=VMEM,
        scratch_shapes=[pltpu.VMEM((3,) + q.shape[1:], BF), pltpu.SemaphoreType.DMA((3,))],
        compiler_params=params(56),
        cost_estimate=pl.CostEstimate(flops=0, bytes_accessed=20 << 20, transcendentals=0),
    )(q, k, v, after)


def keys_kernel(heads_ref, *refs):
    refs[-1][...] = heads_ref[:, 64:192, :]


def keys_of(heads, after):
    return pl.pallas_call(
        keys_kernel,
        out_shape=jax.ShapeDtypeStruct((16, 128, 128), BF),
        in_specs=[VMEM] + [ANY] * len(after),
        out_specs=VMEM,
        compiler_params=params(4),
    )(heads, *after)


def attention_kernel(core_ref, own_ref, oth_ref, out_ref):
    core = core_ref[0]
    queries = own_ref[:, 0:64, :].reshape(1024, 128)
    own_keys = own_ref[:, 64:128, :].reshape(1024, 128)
    own_values = own_ref[:, 128:192, :].reshape(1024, 128)
    oth_keys = oth_ref[:, 0:64, :].reshape(1024, 128)
    oth_values = oth_ref[:, 64:128, :].reshape(1024, 128)
    scale = (HEAD_DIM ** (-0.5)) * LOG2E
    rows = 256
    row = lax.broadcasted_iota(jnp.int32, (rows, rows), 0)
    col = lax.broadcasted_iota(jnp.int32, (rows, rows), 1)
    own_allowed = col <= row
    oth_allowed = (col // 64) < (row // 64) + core
    contract = (((1,), (1,)), ((), ()))
    for j in range(1024 // rows):
        q = queries[j * rows : (j + 1) * rows]
        n = j * rows
        pieces = []
        for keys, values, allowed in (
            (own_keys, own_values, own_allowed),
            (oth_keys, oth_values, oth_allowed),
        ):
            if n:
                s = lax.dot_general(q, keys[:n], contract, preferred_element_type=F32) * scale
                pieces.append((s, values[:n]))
            s = lax.dot_general(q, keys[n : n + rows], contract, preferred_element_type=F32) * scale
            pieces.append((jnp.where(allowed, s, NEG_FILL), values[n : n + rows]))
        top = functools.reduce(jnp.maximum, [jnp.max(s, axis=1, keepdims=True) for s, _ in pieces])
        acc = jnp.zeros((rows, HEAD_DIM), F32)
        total = jnp.zeros((rows, 1), F32)
        for s, values in pieces:
            e = jnp.exp2(s - top)
            total = total + jnp.sum(e, axis=1, keepdims=True)
            acc = acc + jnp.dot(e.astype(BF), values, preferred_element_type=F32)
        out_ref[j * (rows // 64) : (j + 1) * (rows // 64)] = (
            (acc / total).astype(BF).reshape(rows // 64, 64, HEAD_DIM)
        )


def attention(core, own, oth):
    return pl.pallas_call(
        attention_kernel,
        out_shape=jax.ShapeDtypeStruct((16, 64, 128), BF),
        in_specs=[SMEM, VMEM, VMEM],
        out_specs=VMEM,
        compiler_params=params(20),
        cost_estimate=pl.CostEstimate(
            flops=2 * 2 * 1024 * 1280 * 128, bytes_accessed=2 << 20, transcendentals=1024 * 1280
        ),
    )(core, own, oth)


def middle_kernel(where_ref, ctx_ref, *refs):
    pieces, refs = refs[:8], refs[8:]
    res_ref, router_ref, ids_ref, hidden_ref, out_ref, gate_ref, target_ref = refs[:7]
    halves, proj = refs[7:]
    own, place = where_ref[0], (where_ref[1], where_ref[2])
    for n in range(8):
        core = own if n < 4 else 1 - own
        for first in range(4):
            along = (place[0] + jnp.where(core == 0, first, n % 4)) % 4
            across = (place[1] + jnp.where(core == 0, n % 4, first)) % 4
            proj[core, along * 4 + across] = pieces[n][first]
    for h in range(HEADS):
        for c in range(2):
            halves[c * 64 : (c + 1) * 64, h * 128 : (h + 1) * 128] = ctx_ref[h * 2 + c]
    attn = jnp.dot(halves[...], proj[...].reshape(1024, 1024), preferred_element_type=F32)
    hidden = (res_ref[0].astype(F32) + attn).astype(BF)
    hidden_ref[...] = hidden
    wide = hidden.astype(F32)
    mean_square = jnp.mean(wide * wide, axis=1, keepdims=True)
    normed = (wide * lax.rsqrt(mean_square + 1e-06)).astype(BF)
    affinity = jax.nn.sigmoid(
        lax.dot_general(
            router_ref[...], normed, (((1,), (1,)), ((), ())), preferred_element_type=F32
        )
    )
    experts, tokens = affinity.shape
    expert = lax.broadcasted_iota(jnp.int32, (experts, tokens), 0)
    hot = [expert == ids_ref[k : k + 1, :] for k in range(TOP)]
    picked = [jnp.sum(jnp.where(m, affinity, 0.0), axis=0, keepdims=True) for m in hot]
    whole = picked[0] + picked[1]
    before = (
        lax.broadcasted_iota(jnp.int32, (tokens, tokens), 0)
        < lax.broadcasted_iota(jnp.int32, (tokens, tokens), 1)
    ).astype(F32).astype(BF)
    counts = jnp.zeros((experts, 1), F32)
    slot_row = lax.broadcasted_iota(jnp.int32, (experts * SLOT, tokens), 0)
    dispatch = jnp.zeros((experts * SLOT, tokens), F32)
    for k in range(TOP):
        one = hot[k].astype(F32)
        rank = jnp.dot(one.astype(BF), before, preferred_element_type=F32) + counts
        slot = jnp.sum(rank * one, axis=0, keepdims=True).astype(jnp.int32)
        counts = counts + jnp.sum(one, axis=1, keepdims=True)
        target = ids_ref[k : k + 1, :] * SLOT + slot
        dispatch = dispatch + (slot_row == target).astype(F32)
        gate_ref[k : k + 1, :] = picked[k] / whole
        target_ref[k : k + 1, :] = target
    out_ref[...] = jnp.dot(dispatch.astype(BF), normed, preferred_element_type=F32).astype(BF)


def middle(where, ctx, own, oth, residual, router, ids):
    tokens, width = residual.shape[1:]
    experts = router.shape[1]
    return pl.pallas_call(
        middle_kernel,
        out_shape=(
            jax.ShapeDtypeStruct((tokens, width), BF),
            jax.ShapeDtypeStruct((experts * SLOT, width), BF),
            jax.ShapeDtypeStruct((TOP, tokens), F32),
            jax.ShapeDtypeStruct((TOP, tokens), jnp.int32),
        ),
        in_specs=[SMEM] + [VMEM] * 12,
        out_specs=(VMEM,) * 4,
        scratch_shapes=[
            pltpu.VMEM((128, 1024), BF),
            pltpu.VMEM((2, 16, 32, 1024), BF),
        ],
        compiler_params=params(16),
        cost_estimate=pl.CostEstimate(
            flops=2 * 128 * 1024 * 1600, bytes_accessed=4 << 20, transcendentals=4096
        ),
    )(where, ctx, *own, *oth, residual, router.T, ids[0].T)


def pick_kernel(flip, core_ref, weights_ref, after_ref, *refs):
    sems = refs[-1]
    core = core_ref[0]
    first = ((1 - core) if flip else core) * 8
    copies = []
    for n, ref in enumerate(refs[:-1]):
        copies.append(
            pltpu.make_async_copy(weights_ref.at[pl.ds(first, ref.shape[0])], ref, sems.at[n])
        )
        first = first + ref.shape[0]
    for copy in copies:
        copy.start()
    for copy in copies:
        copy.wait()


def pick(core, weights, after, flip, parts):
    return pl.pallas_call(
        functools.partial(pick_kernel, flip),
        out_shape=tuple(jax.ShapeDtypeStruct((n,) + weights.shape[1:], BF) for n in parts),
        in_specs=[SMEM, HBM, ANY],
        out_specs=(VMEM,) * len(parts),
        scratch_shapes=[pltpu.SemaphoreType.DMA((len(parts),))],
        compiler_params=params(52 if flip else 40),
        cost_estimate=pl.CostEstimate(flops=0, bytes_accessed=8 << 20, transcendentals=0),
    )(core, weights, after)


def expert_kernel(core_ref, x_ref, own_ref, *refs):
    oth_refs, (out_ref, up, down) = refs[: len(PARTS)], refs[len(PARTS) :]
    core = core_ref[0]
    pieces = [(own_ref, slice(0, 8), core)]
    first = 0
    for ref in oth_refs:
        pieces.append((ref, slice(first, first + ref.shape[0]), 1 - core))
        first += ref.shape[0]
    for source, z, place in pieces:
        up[z, place, :, 0:1024] = source[:, 0:64, :]
        up[z, place, 0:32, 1024:1536] = source[:, 64:96, 0:512]
        up[z, place, 32:64, 1024:1536] = source[:, 64:96, 512:1024]
        down[z, place] = source[:, 96:144, :]
    ff = down.shape[0] * 2 * down.shape[2]
    inner = jnp.dot(x_ref[...], up[...].reshape(1024, 2 * ff), preferred_element_type=F32)
    activation = (jax.nn.silu(inner[:, :ff]) * inner[:, ff:]).astype(BF)
    out_ref[...] = jnp.dot(
        activation, down[...].reshape(ff, 1024), preferred_element_type=F32
    ).astype(BF)


def experts(core, x, own, oth):
    rows = x.shape[0]
    return pl.pallas_call(
        expert_kernel,
        out_shape=jax.ShapeDtypeStruct((rows, 1024), BF),
        in_specs=[SMEM, VMEM, VMEM] + [VMEM] * len(oth),
        out_specs=VMEM,
        scratch_shapes=[
            pltpu.VMEM((8, 2, 64, 1536), BF),
            pltpu.VMEM((8, 2, 48, 1024), BF),
        ],
        compiler_params=params(24),
        cost_estimate=pl.CostEstimate(
            flops=2 * rows * 1024 * 2304, bytes_accessed=7 << 20, transcendentals=rows * 768
        ),
    )(core, x, own, *oth)


def combine_kernel(back_ref, hidden_ref, gate_ref, target_ref, out_ref):
    tokens = hidden_ref.shape[0]
    slot_row = lax.broadcasted_iota(jnp.int32, (back_ref.shape[0], tokens), 0)
    pad = jnp.zeros((8 - TOP, tokens), F32)
    gates = jnp.transpose(jnp.concatenate([gate_ref[...], pad], axis=0))
    total = hidden_ref[...].astype(F32)
    moe = None
    for k in range(TOP):
        choose = (slot_row == target_ref[k : k + 1, :]).astype(F32).astype(BF)
        pair = lax.dot_general(
            choose, back_ref[...], (((0,), (0,)), ((), ())), preferred_element_type=F32
        ) * gates[:, k : k + 1]
        moe = pair if moe is None else moe + pair
    out_ref[0] = (total + moe).astype(BF)


def combine(back, hidden, gate, target):
    return pl.pallas_call(
        combine_kernel,
        out_shape=jax.ShapeDtypeStruct((1,) + hidden.shape, BF),
        in_specs=[VMEM] * 4,
        out_specs=VMEM,
        compiler_params=params(16),
    )(back, hidden, gate, target)


def on_device(
    residual, query_rows, key_rows, value_rows, out_proj, router, expert_ids,
    expert_gate_up, expert_down,
):
    core_index = lax.axis_index("core")
    core = core_index.astype(jnp.int32).reshape(1)
    packed = pack_weights(expert_gate_up, expert_down)
    weights = lax.all_gather(packed, ("zhi", "zlo"), axis=0, tiled=False)

    moved = lax.ppermute(out_proj, ALL, HALF_MOVE)
    shard = jnp.where(lax.axis_index("zhi") == core_index, out_proj, moved)
    line = jnp.stack([shard] + [lax.ppermute(shard, ALL, plane_pairs(0, d)) for d in (1, 2, 3)])
    proj_own = [line] + [lax.ppermute(line, ALL, plane_pairs(1, d)) for d in (1, 2, 3)]

    heads = pack_heads(query_rows, key_rows, value_rows, moved)
    heads = lax.all_to_all(heads, ("zlo", "core"), split_axis=0, concat_axis=0, tiled=True)
    oth_keys = lax.ppermute(keys_of(heads, proj_own), ALL, CORE_SWAP)
    proj_oth = [lax.ppermute(p, ALL, CORE_SWAP) for p in proj_own]
    context = attention(core, heads, oth_keys)
    context = lax.all_to_all(context, ("zlo", "core"), split_axis=0, concat_axis=0, tiled=True)

    xy = lax.axis_index("xy").astype(jnp.int32).reshape(1)
    where = jnp.concatenate([core, xy // 4, xy % 4])
    hidden, outgoing, gate, target = middle(
        where, context, proj_own, proj_oth, residual, router, expert_ids
    )
    arrived = lax.all_to_all(
        outgoing.reshape(32, SLOT, 1024), ("core", "xy"), split_axis=0, concat_axis=0, tiled=True
    )
    to_send = pick(core, weights, target, True, PARTS)
    oth_weights = [lax.ppermute(w, ALL, CORE_SWAP) for w in to_send]
    (own_weights,) = pick(core, weights, target, False, (8,))
    produced = experts(core, arrived.reshape(32 * SLOT, 1024), own_weights, oth_weights)
    back = lax.all_to_all(
        produced.reshape(32, SLOT, 1024), ("core", "xy"), split_axis=0, concat_axis=0, tiled=True
    )
    return combine(back.reshape(32 * SLOT, 1024), hidden, gate, target)


def solution(mesh):
    fine = Mesh(mesh.devices.reshape(8, 2, 2, 16), ALL)
    rows = P(("zhi", "xy"), ("zlo", "core"), None)
    return jax.shard_map(
        on_device,
        mesh=fine,
        in_specs=(rows, rows, rows, rows, P(("zhi", "xy"), None), P(), rows, rows, rows),
        out_specs=rows,
        check_vma=False,
    )
```

```python
import functools

import jax
import jax.numpy as jnp
from jax import lax
from jax.experimental import pallas as pl
from jax.experimental.pallas import tpu as pltpu
from jax.sharding import Mesh, PartitionSpec as P

HEADS = 8
HEAD_DIM = 128
TOP = 2
SLOT = 16
PARTS = (3, 3, 2)
NEG_FILL = -1e30
LOG2E = 1.4426950408889634
BF = jnp.bfloat16
F32 = jnp.float32
ALL = ("zlo", "core", "zhi", "xy")

VMEM = pl.BlockSpec(memory_space=pltpu.VMEM)
SMEM = pl.BlockSpec(memory_space=pltpu.SMEM)
ANY = pl.BlockSpec(memory_space=pl.ANY)
HBM = pl.BlockSpec(memory_space=pltpu.HBM)


def linear(zlo, core, zhi, xy):
    return ((zlo * 2 + core) * 2 + zhi) * 16 + xy


def all_pairs(move):
    pairs = []
    for zlo in range(8):
        for core in range(2):
            for zhi in range(2):
                for xy in range(16):
                    target = move(zlo, core, zhi, xy)
                    if target is not None:
                        pairs.append((linear(zlo, core, zhi, xy), linear(*target)))
    return pairs


CORE_SWAP = all_pairs(lambda zlo, core, zhi, xy: (zlo, 1 - core, zhi, xy))
HALF_MOVE = all_pairs(
    lambda zlo, core, zhi, xy: (7 - zlo, core, 1 - zhi, xy) if zhi == core else None
)


def plane_pairs(phase, step):
    def move(zlo, core, zhi, xy):
        x, y = divmod(xy, 4)
        if (phase + core) % 2 == 0:
            x = (x - step) % 4
        else:
            y = (y - step) % 4
        return zlo, core, zhi, x * 4 + y

    return all_pairs(move)


def params(mib):
    return pltpu.CompilerParams(vmem_limit_bytes=mib << 20)


def pack_weights_kernel(up_ref, down_ref, out_ref, up, down, sems):
    copies = [
        pltpu.make_async_copy(up_ref.at[0], up, sems.at[0]),
        pltpu.make_async_copy(down_ref.at[0], down, sems.at[1]),
    ]
    for copy in copies:
        copy.start()
    for copy in copies:
        copy.wait()
    out_ref[0:64, :] = up[:, 0:1024]
    out_ref[64:96, 0:512] = up[0:32, 1024:1536]
    out_ref[64:96, 512:1024] = up[32:64, 1024:1536]
    out_ref[96:144, :] = down[...]


def pack_weights(gate_up, down):
    return pl.pallas_call(
        pack_weights_kernel,
        out_shape=jax.ShapeDtypeStruct((144, 1024), BF),
        in_specs=[HBM, HBM],
        out_specs=VMEM,
        scratch_shapes=[
            pltpu.VMEM(gate_up.shape[1:], BF),
            pltpu.VMEM(down.shape[1:], BF),
            pltpu.SemaphoreType.DMA((2,)),
        ],
        compiler_params=params(56),
    )(gate_up, down)


def pack_heads_kernel(q_ref, k_ref, v_ref, out_ref, rows, sems):
    copies = [
        pltpu.make_async_copy(ref.at[0], rows.at[j], sems.at[j])
        for j, ref in enumerate((q_ref, k_ref, v_ref))
    ]
    for copy in copies:
        copy.start()
    for j, copy in enumerate(copies):
        copy.wait()
        for h in range(HEADS):
            for c in range(2):
                out_ref[h * 2 + c, j * 64 : (j + 1) * 64, :] = rows[
                    j, c * 64 : (c + 1) * 64, h * 128 : (h + 1) * 128
                ]


def pack_heads(q, k, v):
    return pl.pallas_call(
        pack_heads_kernel,
        out_shape=jax.ShapeDtypeStruct((16, 192, 128), BF),
        in_specs=[HBM] * 3,
        out_specs=VMEM,
        scratch_shapes=[pltpu.VMEM((3,) + q.shape[1:], BF), pltpu.SemaphoreType.DMA((3,))],
        compiler_params=params(56),
        cost_estimate=pl.CostEstimate(flops=0, bytes_accessed=20 << 20, transcendentals=0),
    )(q, k, v)


def keys_kernel(heads_ref, *refs):
    refs[-1][...] = heads_ref[:, 64:192, :]


def keys_of(heads, after):
    return pl.pallas_call(
        keys_kernel,
        out_shape=jax.ShapeDtypeStruct((16, 128, 128), BF),
        in_specs=[VMEM] + [ANY] * len(after),
        out_specs=VMEM,
        compiler_params=params(4),
    )(heads, *after)


def line_kernel(*refs):
    for n, ref in enumerate(refs[:4]):
        refs[-1][n] = ref[...]


def line_of(pieces, after):
    return pl.pallas_call(
        line_kernel,
        out_shape=jax.ShapeDtypeStruct((4,) + pieces[0].shape, BF),
        in_specs=[VMEM] * 4 + [ANY],
        out_specs=VMEM,
        compiler_params=params(4),
    )(*pieces, after)


def attention_kernel(core_ref, own_ref, oth_ref, out_ref):
    core = core_ref[0]
    queries = own_ref[:, 0:64, :].reshape(1024, 128)
    own_keys = own_ref[:, 64:128, :].reshape(1024, 128)
    own_values = own_ref[:, 128:192, :].reshape(1024, 128)
    oth_keys = oth_ref[:, 0:64, :].reshape(1024, 128)
    oth_values = oth_ref[:, 64:128, :].reshape(1024, 128)
    scale = (HEAD_DIM ** (-0.5)) * LOG2E
    rows = 256
    row = lax.broadcasted_iota(jnp.int32, (rows, rows), 0)
    col = lax.broadcasted_iota(jnp.int32, (rows, rows), 1)
    own_allowed = col <= row
    oth_allowed = (col // 64) < (row // 64) + core
    contract = (((1,), (1,)), ((), ()))
    for j in range(1024 // rows):
        q = queries[j * rows : (j + 1) * rows]
        n = j * rows
        pieces = []
        for keys, values, allowed in (
            (own_keys, own_values, own_allowed),
            (oth_keys, oth_values, oth_allowed),
        ):
            if n:
                s = lax.dot_general(q, keys[:n], contract, preferred_element_type=F32) * scale
                pieces.append((s, values[:n]))
            s = lax.dot_general(q, keys[n : n + rows], contract, preferred_element_type=F32) * scale
            pieces.append((jnp.where(allowed, s, NEG_FILL), values[n : n + rows]))
        top = functools.reduce(jnp.maximum, [jnp.max(s, axis=1, keepdims=True) for s, _ in pieces])
        acc = jnp.zeros((rows, HEAD_DIM), F32)
        total = jnp.zeros((rows, 1), F32)
        for s, values in pieces:
            e = jnp.exp2(s - top)
            total = total + jnp.sum(e, axis=1, keepdims=True)
            acc = acc + jnp.dot(e.astype(BF), values, preferred_element_type=F32)
        out_ref[j * (rows // 64) : (j + 1) * (rows // 64)] = (
            (acc / total).astype(BF).reshape(rows // 64, 64, HEAD_DIM)
        )


def attention(core, own, oth):
    return pl.pallas_call(
        attention_kernel,
        out_shape=jax.ShapeDtypeStruct((16, 64, 128), BF),
        in_specs=[SMEM, VMEM, VMEM],
        out_specs=VMEM,
        compiler_params=params(20),
        cost_estimate=pl.CostEstimate(
            flops=2 * 2 * 1024 * 1280 * 128, bytes_accessed=2 << 20, transcendentals=1024 * 1280
        ),
    )(core, own, oth)


def middle_kernel(where_ref, ctx_ref, *refs):
    pieces, refs = refs[:8], refs[8:]
    res_ref, router_ref, ids_ref, hidden_ref, out_ref, gate_ref, target_ref = refs[:7]
    halves, proj = refs[7:]
    own, place = where_ref[0], (where_ref[1], where_ref[2])
    for n in range(8):
        core = own if n < 4 else 1 - own
        for first in range(4):
            along = (place[0] + jnp.where(core == 0, first, n % 4)) % 4
            across = (place[1] + jnp.where(core == 0, n % 4, first)) % 4
            proj[core, along * 4 + across] = pieces[n][first]
    for h in range(HEADS):
        for c in range(2):
            halves[c * 64 : (c + 1) * 64, h * 128 : (h + 1) * 128] = ctx_ref[h * 2 + c]
    attn = jnp.dot(halves[...], proj[...].reshape(1024, 1024), preferred_element_type=F32)
    hidden = (res_ref[0].astype(F32) + attn).astype(BF)
    hidden_ref[...] = hidden
    wide = hidden.astype(F32)
    mean_square = jnp.mean(wide * wide, axis=1, keepdims=True)
    normed = (wide * lax.rsqrt(mean_square + 1e-06)).astype(BF)
    affinity = jax.nn.sigmoid(
        lax.dot_general(
            router_ref[...], normed, (((1,), (1,)), ((), ())), preferred_element_type=F32
        )
    )
    experts, tokens = affinity.shape
    expert = lax.broadcasted_iota(jnp.int32, (experts, tokens), 0)
    hot = [expert == ids_ref[k : k + 1, :] for k in range(TOP)]
    picked = [jnp.sum(jnp.where(m, affinity, 0.0), axis=0, keepdims=True) for m in hot]
    whole = picked[0] + picked[1]
    before = (
        lax.broadcasted_iota(jnp.int32, (tokens, tokens), 0)
        < lax.broadcasted_iota(jnp.int32, (tokens, tokens), 1)
    ).astype(F32).astype(BF)
    counts = jnp.zeros((experts, 1), F32)
    slot_row = lax.broadcasted_iota(jnp.int32, (experts * SLOT, tokens), 0)
    dispatch = jnp.zeros((experts * SLOT, tokens), F32)
    for k in range(TOP):
        one = hot[k].astype(F32)
        rank = jnp.dot(one.astype(BF), before, preferred_element_type=F32) + counts
        slot = jnp.sum(rank * one, axis=0, keepdims=True).astype(jnp.int32)
        counts = counts + jnp.sum(one, axis=1, keepdims=True)
        target = ids_ref[k : k + 1, :] * SLOT + slot
        dispatch = dispatch + (slot_row == target).astype(F32)
        gate_ref[k : k + 1, :] = picked[k] / whole
        target_ref[k : k + 1, :] = target
    out_ref[...] = jnp.dot(dispatch.astype(BF), normed, preferred_element_type=F32).astype(BF)


def middle(where, ctx, own, oth, residual, router, ids):
    tokens, width = residual.shape[1:]
    experts = router.shape[1]
    return pl.pallas_call(
        middle_kernel,
        out_shape=(
            jax.ShapeDtypeStruct((tokens, width), BF),
            jax.ShapeDtypeStruct((experts * SLOT, width), BF),
            jax.ShapeDtypeStruct((TOP, tokens), F32),
            jax.ShapeDtypeStruct((TOP, tokens), jnp.int32),
        ),
        in_specs=[SMEM] + [VMEM] * 12,
        out_specs=(VMEM,) * 4,
        scratch_shapes=[
            pltpu.VMEM((128, 1024), BF),
            pltpu.VMEM((2, 16, 32, 1024), BF),
        ],
        compiler_params=params(16),
        cost_estimate=pl.CostEstimate(
            flops=2 * 128 * 1024 * 1600, bytes_accessed=4 << 20, transcendentals=4096
        ),
    )(where, ctx, *own, *oth, residual, router.T, ids[0].T)


def pick_kernel(flip, core_ref, weights_ref, after_ref, *refs):
    sems = refs[-1]
    core = core_ref[0]
    first = ((1 - core) if flip else core) * 8
    copies = []
    for n, ref in enumerate(refs[:-1]):
        copies.append(
            pltpu.make_async_copy(weights_ref.at[pl.ds(first, ref.shape[0])], ref, sems.at[n])
        )
        first = first + ref.shape[0]
    for copy in copies:
        copy.start()
    for copy in copies:
        copy.wait()


def pick(core, weights, after, flip, parts):
    return pl.pallas_call(
        functools.partial(pick_kernel, flip),
        out_shape=tuple(jax.ShapeDtypeStruct((n,) + weights.shape[1:], BF) for n in parts),
        in_specs=[SMEM, HBM, ANY],
        out_specs=(VMEM,) * len(parts),
        scratch_shapes=[pltpu.SemaphoreType.DMA((len(parts),))],
        compiler_params=params(52 if flip else 40),
        cost_estimate=pl.CostEstimate(flops=0, bytes_accessed=8 << 20, transcendentals=0),
    )(core, weights, after)


def expert_kernel(core_ref, x_ref, own_ref, *refs):
    oth_refs, (out_ref, up, down) = refs[: len(PARTS)], refs[len(PARTS) :]
    core = core_ref[0]
    pieces = [(own_ref, slice(0, 8), core)]
    first = 0
    for ref in oth_refs:
        pieces.append((ref, slice(first, first + ref.shape[0]), 1 - core))
        first += ref.shape[0]
    for source, z, place in pieces:
        up[z, place, :, 0:1024] = source[:, 0:64, :]
        up[z, place, 0:32, 1024:1536] = source[:, 64:96, 0:512]
        up[z, place, 32:64, 1024:1536] = source[:, 64:96, 512:1024]
        down[z, place] = source[:, 96:144, :]
    ff = down.shape[0] * 2 * down.shape[2]
    inner = jnp.dot(x_ref[...], up[...].reshape(1024, 2 * ff), preferred_element_type=F32)
    activation = (jax.nn.silu(inner[:, :ff]) * inner[:, ff:]).astype(BF)
    out_ref[...] = jnp.dot(
        activation, down[...].reshape(ff, 1024), preferred_element_type=F32
    ).astype(BF)


def experts(core, x, own, oth):
    rows = x.shape[0]
    return pl.pallas_call(
        expert_kernel,
        out_shape=jax.ShapeDtypeStruct((rows, 1024), BF),
        in_specs=[SMEM, VMEM, VMEM] + [VMEM] * len(oth),
        out_specs=VMEM,
        scratch_shapes=[
            pltpu.VMEM((8, 2, 64, 1536), BF),
            pltpu.VMEM((8, 2, 48, 1024), BF),
        ],
        compiler_params=params(24),
        cost_estimate=pl.CostEstimate(
            flops=2 * rows * 1024 * 2304, bytes_accessed=7 << 20, transcendentals=rows * 768
        ),
    )(core, x, own, *oth)


def combine_kernel(back_ref, hidden_ref, gate_ref, target_ref, out_ref):
    tokens = hidden_ref.shape[0]
    slot_row = lax.broadcasted_iota(jnp.int32, (back_ref.shape[0], tokens), 0)
    pad = jnp.zeros((8 - TOP, tokens), F32)
    gates = jnp.transpose(jnp.concatenate([gate_ref[...], pad], axis=0))
    total = hidden_ref[...].astype(F32)
    moe = None
    for k in range(TOP):
        choose = (slot_row == target_ref[k : k + 1, :]).astype(F32).astype(BF)
        pair = lax.dot_general(
            choose, back_ref[...], (((0,), (0,)), ((), ())), preferred_element_type=F32
        ) * gates[:, k : k + 1]
        moe = pair if moe is None else moe + pair
    out_ref[0] = (total + moe).astype(BF)


def combine(back, hidden, gate, target):
    return pl.pallas_call(
        combine_kernel,
        out_shape=jax.ShapeDtypeStruct((1,) + hidden.shape, BF),
        in_specs=[VMEM] * 4,
        out_specs=VMEM,
        compiler_params=params(16),
    )(back, hidden, gate, target)


def on_device(
    residual, query_rows, key_rows, value_rows, out_proj, router, expert_ids,
    expert_gate_up, expert_down,
):
    core_index = lax.axis_index("core")
    core = core_index.astype(jnp.int32).reshape(1)
    packed = pack_weights(expert_gate_up, expert_down)
    weights = lax.all_gather(packed, ("zhi", "zlo"), axis=0, tiled=False)

    moved = lax.ppermute(out_proj, ALL, HALF_MOVE)
    shard = jnp.where(lax.axis_index("zhi") == core_index, out_proj, moved)
    pieces = [shard] + [lax.ppermute(shard, ALL, plane_pairs(0, d)) for d in (1, 2, 3)]

    heads = pack_heads(query_rows, key_rows, value_rows)
    heads = lax.all_to_all(heads, ("zlo", "core"), split_axis=0, concat_axis=0, tiled=True)
    oth_keys = lax.ppermute(keys_of(heads, pieces), ALL, CORE_SWAP)
    context = attention(core, heads, oth_keys)

    line = line_of(pieces, context)
    proj_own = [line] + [lax.ppermute(line, ALL, plane_pairs(1, d)) for d in (1, 2, 3)]
    proj_oth = [lax.ppermute(p, ALL, CORE_SWAP) for p in proj_own]
    context = lax.all_to_all(context, ("zlo", "core"), split_axis=0, concat_axis=0, tiled=True)

    xy = lax.axis_index("xy").astype(jnp.int32).reshape(1)
    where = jnp.concatenate([core, xy // 4, xy % 4])
    hidden, outgoing, gate, target = middle(
        where, context, proj_own, proj_oth, residual, router, expert_ids
    )
    arrived = lax.all_to_all(
        outgoing.reshape(32, SLOT, 1024), ("core", "xy"), split_axis=0, concat_axis=0, tiled=True
    )
    to_send = pick(core, weights, target, True, PARTS)
    oth_weights = [lax.ppermute(w, ALL, CORE_SWAP) for w in to_send]
    (own_weights,) = pick(core, weights, target, False, (8,))
    produced = experts(core, arrived.reshape(32 * SLOT, 1024), own_weights, oth_weights)
    back = lax.all_to_all(
        produced.reshape(32, SLOT, 1024), ("core", "xy"), split_axis=0, concat_axis=0, tiled=True
    )
    return combine(back.reshape(32 * SLOT, 1024), hidden, gate, target)


def solution(mesh):
    fine = Mesh(mesh.devices.reshape(8, 2, 2, 16), ALL)
    rows = P(("zhi", "xy"), ("zlo", "core"), None)
    return jax.shard_map(
        on_device,
        mesh=fine,
        in_specs=(rows, rows, rows, rows, P(("zhi", "xy"), None), P(), rows, rows, rows),
        out_specs=rows,
        check_vma=False,
    )
```

```python
import functools

import jax
import jax.numpy as jnp
from jax import lax
from jax.experimental import pallas as pl
from jax.experimental.pallas import tpu as pltpu
from jax.sharding import Mesh, PartitionSpec as P

HEADS = 8
HEAD_DIM = 128
TOP = 2
SLOT = 16
PARTS = (3, 3, 2)
NEG_FILL = -1e30
LOG2E = 1.4426950408889634
BF = jnp.bfloat16
F32 = jnp.float32
ALL = ("zlo", "core", "zhi", "xy")

VMEM = pl.BlockSpec(memory_space=pltpu.VMEM)
SMEM = pl.BlockSpec(memory_space=pltpu.SMEM)
ANY = pl.BlockSpec(memory_space=pl.ANY)
HBM = pl.BlockSpec(memory_space=pltpu.HBM)


def linear(zlo, core, zhi, xy):
    return ((zlo * 2 + core) * 2 + zhi) * 16 + xy


def all_pairs(move):
    pairs = []
    for zlo in range(8):
        for core in range(2):
            for zhi in range(2):
                for xy in range(16):
                    target = move(zlo, core, zhi, xy)
                    if target is not None:
                        pairs.append((linear(zlo, core, zhi, xy), linear(*target)))
    return pairs


CORE_SWAP = all_pairs(lambda zlo, core, zhi, xy: (zlo, 1 - core, zhi, xy))
HALF_MOVE = all_pairs(
    lambda zlo, core, zhi, xy: (7 - zlo, core, 1 - zhi, xy) if zhi == core else None
)


def plane_pairs(phase, step):
    def move(zlo, core, zhi, xy):
        x, y = divmod(xy, 4)
        if (phase + core) % 2 == 0:
            x = (x - step) % 4
        else:
            y = (y - step) % 4
        return zlo, core, zhi, x * 4 + y

    return all_pairs(move)


def params(mib):
    return pltpu.CompilerParams(vmem_limit_bytes=mib << 20)


def pack_weights_kernel(up_ref, down_ref, out_ref, up, down, sems):
    copies = [
        pltpu.make_async_copy(up_ref.at[0], up, sems.at[0]),
        pltpu.make_async_copy(down_ref.at[0], down, sems.at[1]),
    ]
    for copy in copies:
        copy.start()
    for copy in copies:
        copy.wait()
    out_ref[0:64, :] = up[:, 0:1024]
    out_ref[64:96, 0:512] = up[0:32, 1024:1536]
    out_ref[64:96, 512:1024] = up[32:64, 1024:1536]
    out_ref[96:144, :] = down[...]


def pack_weights(gate_up, down):
    return pl.pallas_call(
        pack_weights_kernel,
        out_shape=jax.ShapeDtypeStruct((144, 1024), BF),
        in_specs=[HBM, HBM],
        out_specs=VMEM,
        scratch_shapes=[
            pltpu.VMEM(gate_up.shape[1:], BF),
            pltpu.VMEM(down.shape[1:], BF),
            pltpu.SemaphoreType.DMA((2,)),
        ],
        compiler_params=params(56),
    )(gate_up, down)


def pack_heads_kernel(q_ref, k_ref, v_ref, out_ref, rows, sems):
    copies = [
        pltpu.make_async_copy(ref.at[0], rows.at[j], sems.at[j])
        for j, ref in enumerate((q_ref, k_ref, v_ref))
    ]
    for copy in copies:
        copy.start()
    for j, copy in enumerate(copies):
        copy.wait()
        for h in range(HEADS):
            for c in range(2):
                out_ref[h * 2 + c, j * 64 : (j + 1) * 64, :] = rows[
                    j, c * 64 : (c + 1) * 64, h * 128 : (h + 1) * 128
                ]


def pack_heads(q, k, v):
    return pl.pallas_call(
        pack_heads_kernel,
        out_shape=jax.ShapeDtypeStruct((16, 192, 128), BF),
        in_specs=[HBM] * 3,
        out_specs=VMEM,
        scratch_shapes=[pltpu.VMEM((3,) + q.shape[1:], BF), pltpu.SemaphoreType.DMA((3,))],
        compiler_params=params(56),
        cost_estimate=pl.CostEstimate(flops=0, bytes_accessed=20 << 20, transcendentals=0),
    )(q, k, v)


def keys_kernel(heads_ref, *refs):
    refs[-1][...] = heads_ref[:, 64:192, :]


def keys_of(heads, after):
    return pl.pallas_call(
        keys_kernel,
        out_shape=jax.ShapeDtypeStruct((16, 128, 128), BF),
        in_specs=[VMEM] + [ANY] * len(after),
        out_specs=VMEM,
        compiler_params=params(4),
    )(heads, *after)


def line_kernel(*refs):
    for n, ref in enumerate(refs[:4]):
        refs[-1][n] = ref[...]


def line_of(pieces, after):
    return pl.pallas_call(
        line_kernel,
        out_shape=jax.ShapeDtypeStruct((4,) + pieces[0].shape, BF),
        in_specs=[VMEM] * 4 + [ANY],
        out_specs=VMEM,
        compiler_params=params(4),
    )(*pieces, after)


def stack_kernel(*refs):
    for n, ref in enumerate(refs[:-1]):
        refs[-1][n] = ref[...]


def stack(pieces):
    return pl.pallas_call(
        stack_kernel,
        out_shape=jax.ShapeDtypeStruct((len(pieces),) + pieces[0].shape, BF),
        in_specs=[VMEM] * len(pieces),
        out_specs=VMEM,
        compiler_params=params(4),
    )(*pieces)


def attention_kernel(core_ref, own_ref, oth_ref, out_ref):
    core = core_ref[0]
    queries = own_ref[:, 0:64, :].reshape(1024, 128)
    own_keys = own_ref[:, 64:128, :].reshape(1024, 128)
    own_values = own_ref[:, 128:192, :].reshape(1024, 128)
    oth_keys = oth_ref[:, 0:64, :].reshape(1024, 128)
    oth_values = oth_ref[:, 64:128, :].reshape(1024, 128)
    scale = (HEAD_DIM ** (-0.5)) * LOG2E
    rows = 256
    row = lax.broadcasted_iota(jnp.int32, (rows, rows), 0)
    col = lax.broadcasted_iota(jnp.int32, (rows, rows), 1)
    own_allowed = col <= row
    oth_allowed = (col // 64) < (row // 64) + core
    contract = (((1,), (1,)), ((), ()))
    for j in range(1024 // rows):
        q = queries[j * rows : (j + 1) * rows]
        n = j * rows
        pieces = []
        for keys, values, allowed in (
            (own_keys, own_values, own_allowed),
            (oth_keys, oth_values, oth_allowed),
        ):
            if n:
                s = lax.dot_general(q, keys[:n], contract, preferred_element_type=F32) * scale
                pieces.append((s, values[:n]))
            s = lax.dot_general(q, keys[n : n + rows], contract, preferred_element_type=F32) * scale
            pieces.append((jnp.where(allowed, s, NEG_FILL), values[n : n + rows]))
        top = functools.reduce(jnp.maximum, [jnp.max(s, axis=1, keepdims=True) for s, _ in pieces])
        acc = jnp.zeros((rows, HEAD_DIM), F32)
        total = jnp.zeros((rows, 1), F32)
        for s, values in pieces:
            e = jnp.exp2(s - top)
            total = total + jnp.sum(e, axis=1, keepdims=True)
            acc = acc + jnp.dot(e.astype(BF), values, preferred_element_type=F32)
        out_ref[j * (rows // 64) : (j + 1) * (rows // 64)] = (
            (acc / total).astype(BF).reshape(rows // 64, 64, HEAD_DIM)
        )


def attention(core, own, oth):
    return pl.pallas_call(
        attention_kernel,
        out_shape=jax.ShapeDtypeStruct((16, 64, 128), BF),
        in_specs=[SMEM, VMEM, VMEM],
        out_specs=VMEM,
        compiler_params=params(20),
        cost_estimate=pl.CostEstimate(
            flops=2 * 2 * 1024 * 1280 * 128, bytes_accessed=2 << 20, transcendentals=1024 * 1280
        ),
    )(core, own, oth)


def middle_kernel(where_ref, ctx_ref, *refs):
    sides, refs = (refs[:2], refs[2:4]), refs[4:]
    res_ref, router_ref, ids_ref, hidden_ref, out_ref, gate_ref, target_ref = refs[:7]
    halves, proj = refs[7:]
    own, place = where_ref[0], (where_ref[1], where_ref[2])
    for side in range(2):
        core = own if side == 0 else 1 - own
        for second in range(4):
            for first in range(4):
                along = (place[0] + jnp.where(core == 0, first, second)) % 4
                across = (place[1] + jnp.where(core == 0, second, first)) % 4
                proj[core, along * 4 + across] = sides[side][second // 2][second % 2, first]
    for h in range(HEADS):
        for c in range(2):
            halves[c * 64 : (c + 1) * 64, h * 128 : (h + 1) * 128] = ctx_ref[h * 2 + c]
    attn = jnp.dot(halves[...], proj[...].reshape(1024, 1024), preferred_element_type=F32)
    hidden = (res_ref[0].astype(F32) + attn).astype(BF)
    hidden_ref[...] = hidden
    wide = hidden.astype(F32)
    mean_square = jnp.mean(wide * wide, axis=1, keepdims=True)
    normed = (wide * lax.rsqrt(mean_square + 1e-06)).astype(BF)
    affinity = jax.nn.sigmoid(
        lax.dot_general(
            router_ref[...], normed, (((1,), (1,)), ((), ())), preferred_element_type=F32
        )
    )
    experts, tokens = affinity.shape
    expert = lax.broadcasted_iota(jnp.int32, (experts, tokens), 0)
    hot = [expert == ids_ref[k : k + 1, :] for k in range(TOP)]
    picked = [jnp.sum(jnp.where(m, affinity, 0.0), axis=0, keepdims=True) for m in hot]
    whole = picked[0] + picked[1]
    before = (
        lax.broadcasted_iota(jnp.int32, (tokens, tokens), 0)
        < lax.broadcasted_iota(jnp.int32, (tokens, tokens), 1)
    ).astype(F32).astype(BF)
    counts = jnp.zeros((experts, 1), F32)
    slot_row = lax.broadcasted_iota(jnp.int32, (experts * SLOT, tokens), 0)
    dispatch = jnp.zeros((experts * SLOT, tokens), F32)
    for k in range(TOP):
        one = hot[k].astype(F32)
        rank = jnp.dot(one.astype(BF), before, preferred_element_type=F32) + counts
        slot = jnp.sum(rank * one, axis=0, keepdims=True).astype(jnp.int32)
        counts = counts + jnp.sum(one, axis=1, keepdims=True)
        target = ids_ref[k : k + 1, :] * SLOT + slot
        dispatch = dispatch + (slot_row == target).astype(F32)
        gate_ref[k : k + 1, :] = picked[k] / whole
        target_ref[k : k + 1, :] = target
    out_ref[...] = jnp.dot(dispatch.astype(BF), normed, preferred_element_type=F32).astype(BF)


def middle(where, ctx, own, oth, residual, router, ids):
    tokens, width = residual.shape[1:]
    experts = router.shape[1]
    return pl.pallas_call(
        middle_kernel,
        out_shape=(
            jax.ShapeDtypeStruct((tokens, width), BF),
            jax.ShapeDtypeStruct((experts * SLOT, width), BF),
            jax.ShapeDtypeStruct((TOP, tokens), F32),
            jax.ShapeDtypeStruct((TOP, tokens), jnp.int32),
        ),
        in_specs=[SMEM] + [VMEM] * 8,
        out_specs=(VMEM,) * 4,
        scratch_shapes=[
            pltpu.VMEM((128, 1024), BF),
            pltpu.VMEM((2, 16, 32, 1024), BF),
        ],
        compiler_params=params(16),
        cost_estimate=pl.CostEstimate(
            flops=2 * 128 * 1024 * 1600, bytes_accessed=4 << 20, transcendentals=4096
        ),
    )(where, ctx, *own, *oth, residual, router.T, ids[0].T)


def pick_kernel(flip, core_ref, weights_ref, after_ref, *refs):
    sems = refs[-1]
    core = core_ref[0]
    first = ((1 - core) if flip else core) * 8
    copies = []
    for n, ref in enumerate(refs[:-1]):
        copies.append(
            pltpu.make_async_copy(weights_ref.at[pl.ds(first, ref.shape[0])], ref, sems.at[n])
        )
        first = first + ref.shape[0]
    for copy in copies:
        copy.start()
    for copy in copies:
        copy.wait()


def pick(core, weights, after, flip, parts):
    return pl.pallas_call(
        functools.partial(pick_kernel, flip),
        out_shape=tuple(jax.ShapeDtypeStruct((n,) + weights.shape[1:], BF) for n in parts),
        in_specs=[SMEM, HBM, ANY],
        out_specs=(VMEM,) * len(parts),
        scratch_shapes=[pltpu.SemaphoreType.DMA((len(parts),))],
        compiler_params=params(52 if flip else 40),
        cost_estimate=pl.CostEstimate(flops=0, bytes_accessed=8 << 20, transcendentals=0),
    )(core, weights, after)


def expert_kernel(core_ref, x_ref, own_ref, *refs):
    oth_refs, (out_ref, up, down) = refs[: len(PARTS)], refs[len(PARTS) :]
    core = core_ref[0]
    pieces = [(own_ref, slice(0, 8), core)]
    first = 0
    for ref in oth_refs:
        pieces.append((ref, slice(first, first + ref.shape[0]), 1 - core))
        first += ref.shape[0]
    for source, z, place in pieces:
        up[z, place, :, 0:1024] = source[:, 0:64, :]
        up[z, place, 0:32, 1024:1536] = source[:, 64:96, 0:512]
        up[z, place, 32:64, 1024:1536] = source[:, 64:96, 512:1024]
        down[z, place] = source[:, 96:144, :]
    ff = down.shape[0] * 2 * down.shape[2]
    inner = jnp.dot(x_ref[...], up[...].reshape(1024, 2 * ff), preferred_element_type=F32)
    activation = (jax.nn.silu(inner[:, :ff]) * inner[:, ff:]).astype(BF)
    out_ref[...] = jnp.dot(
        activation, down[...].reshape(ff, 1024), preferred_element_type=F32
    ).astype(BF)


def experts(core, x, own, oth):
    rows = x.shape[0]
    return pl.pallas_call(
        expert_kernel,
        out_shape=jax.ShapeDtypeStruct((rows, 1024), BF),
        in_specs=[SMEM, VMEM, VMEM] + [VMEM] * len(oth),
        out_specs=VMEM,
        scratch_shapes=[
            pltpu.VMEM((8, 2, 64, 1536), BF),
            pltpu.VMEM((8, 2, 48, 1024), BF),
        ],
        compiler_params=params(24),
        cost_estimate=pl.CostEstimate(
            flops=2 * rows * 1024 * 2304, bytes_accessed=7 << 20, transcendentals=rows * 768
        ),
    )(core, x, own, *oth)


def combine_kernel(back_ref, hidden_ref, gate_ref, target_ref, out_ref):
    tokens = hidden_ref.shape[0]
    slot_row = lax.broadcasted_iota(jnp.int32, (back_ref.shape[0], tokens), 0)
    pad = jnp.zeros((8 - TOP, tokens), F32)
    gates = jnp.transpose(jnp.concatenate([gate_ref[...], pad], axis=0))
    total = hidden_ref[...].astype(F32)
    moe = None
    for k in range(TOP):
        choose = (slot_row == target_ref[k : k + 1, :]).astype(F32).astype(BF)
        pair = lax.dot_general(
            choose, back_ref[...], (((0,), (0,)), ((), ())), preferred_element_type=F32
        ) * gates[:, k : k + 1]
        moe = pair if moe is None else moe + pair
    out_ref[0] = (total + moe).astype(BF)


def combine(back, hidden, gate, target):
    return pl.pallas_call(
        combine_kernel,
        out_shape=jax.ShapeDtypeStruct((1,) + hidden.shape, BF),
        in_specs=[VMEM] * 4,
        out_specs=VMEM,
        compiler_params=params(16),
    )(back, hidden, gate, target)


def on_device(
    residual, query_rows, key_rows, value_rows, out_proj, router, expert_ids,
    expert_gate_up, expert_down,
):
    core_index = lax.axis_index("core")
    core = core_index.astype(jnp.int32).reshape(1)
    packed = pack_weights(expert_gate_up, expert_down)
    weights = lax.all_gather(packed, ("zhi", "zlo"), axis=0, tiled=False)

    moved = lax.ppermute(out_proj, ALL, HALF_MOVE)
    shard = jnp.where(lax.axis_index("zhi") == core_index, out_proj, moved)
    pieces = [shard] + [lax.ppermute(shard, ALL, plane_pairs(0, d)) for d in (1, 2, 3)]

    heads = pack_heads(query_rows, key_rows, value_rows)
    heads = lax.all_to_all(heads, ("zlo", "core"), split_axis=0, concat_axis=0, tiled=True)
    oth_keys = lax.ppermute(keys_of(heads, pieces), ALL, CORE_SWAP)
    context = attention(core, heads, oth_keys)

    line = line_of(pieces, context)
    lines = [line] + [lax.ppermute(line, ALL, plane_pairs(1, d)) for d in (1, 2, 3)]
    proj_own = [stack(lines[:2]), stack(lines[2:])]
    proj_oth = [lax.ppermute(p, ALL, CORE_SWAP) for p in proj_own]
    context = lax.all_to_all(context, ("zlo", "core"), split_axis=0, concat_axis=0, tiled=True)

    xy = lax.axis_index("xy").astype(jnp.int32).reshape(1)
    where = jnp.concatenate([core, xy // 4, xy % 4])
    hidden, outgoing, gate, target = middle(
        where, context, proj_own, proj_oth, residual, router, expert_ids
    )
    arrived = lax.all_to_all(
        outgoing.reshape(32, SLOT, 1024), ("core", "xy"), split_axis=0, concat_axis=0, tiled=True
    )
    to_send = pick(core, weights, target, True, PARTS)
    oth_weights = [lax.ppermute(w, ALL, CORE_SWAP) for w in to_send]
    (own_weights,) = pick(core, weights, target, False, (8,))
    produced = experts(core, arrived.reshape(32 * SLOT, 1024), own_weights, oth_weights)
    back = lax.all_to_all(
        produced.reshape(32, SLOT, 1024), ("core", "xy"), split_axis=0, concat_axis=0, tiled=True
    )
    return combine(back.reshape(32 * SLOT, 1024), hidden, gate, target)


def solution(mesh):
    fine = Mesh(mesh.devices.reshape(8, 2, 2, 16), ALL)
    rows = P(("zhi", "xy"), ("zlo", "core"), None)
    return jax.shard_map(
        on_device,
        mesh=fine,
        in_specs=(rows, rows, rows, rows, P(("zhi", "xy"), None), P(), rows, rows, rows),
        out_specs=rows,
        check_vma=False,
    )
```
